128 devices in a mesh: section: 4 (over y), vocab: 32 (over x, z, core).
Axes of the slice: x: 4, y: 4, z: 4, core: 2. Of those that a mesh axis runs over, the one named last changes fastest.
Arguments:
- hidden_rows: bfloat16 [1024, 8192], P(('section', 'vocab')), may hold values from -170 to 170
- norm_gain: float32 [8192], replicated, may hold values from 0.5 to 1.5
- head_weight: bfloat16 [8192, 65536], P('section', 'vocab'), may hold values from -1.7 to 1.7
- targets: int32 [1024], P(('section', 'vocab')), may hold values from 0 to 65535
- exit_layer: int32 [4], replicated, may hold values from 0 to 79
- numerators: int32 [80], replicated, may hold values from 1 to 16
Outputs:
- hidden_grad: bfloat16 [1024, 8192], P(('section', 'vocab'))
- gain_grad: float32 [8192], replicated
- head_grad: bfloat16 [8192, 65536], P('section', 'vocab')
- total_loss: float32 [], replicated
The draws below stay inside these ranges and needn't reach their ends.
All inputs are finite; a program needn't handle non-finite values.
Results may differ from the reference program's by a relative error of at most 0.0082.
Values may be sent and summed in bfloat16 or wider, within the bound.
No kernel may reach another device: no remote copies, remote signals or barrier semaphores. Data moves between devices by JAX's collectives and lax.ppermute only.
A program may use at most 128 MiB of HBM per device.

```python
import math
import jax
import jax.numpy as jnp
import numpy as np
from jax import lax

D = 8192
LAYERS = 80
SECTIONS = 4
ROWS = 1024
VOCAB = 65536


def anchor_setup(key):
    place_key, column_key, direction_key = jax.random.split(key, 3)
    rows_at = jax.random.randint(place_key, (3,), 0, ROWS)
    columns_at = jax.random.randint(column_key, (3,), 0, VOCAB)
    directions = jnp.clip(jax.random.normal(direction_key, (3, D), jnp.float32), -6.0, 6.0)
    return (rows_at, columns_at, directions)


def draw_hidden_rows(key, part):
    rows_at, columns_at, directions = anchor_setup(key)
    drawn_key = jax.random.fold_in(key, 11)
    base_key = jax.random.fold_in(drawn_key, 0)
    values = jnp.clip(jax.random.normal(base_key, (ROWS, D), jnp.float32), -6.0, 6.0)
    row_ids = jnp.arange(ROWS, dtype=jnp.int32)[:, None]
    for anchor in range(3):
        values = jnp.where(row_ids == rows_at[anchor], directions[anchor][None, :], values)
    return values.astype(jnp.bfloat16)


def draw_head_weight(key, part):
    rows_at, columns_at, directions = anchor_setup(key)
    drawn_key = jax.random.fold_in(key, 12)
    base_key = jax.random.fold_in(drawn_key, 0)
    column_ids = jnp.arange(VOCAB, dtype=jnp.int32)[None, :]
    feature_ids = jnp.arange(D, dtype=jnp.int32)
    rising = (3.0 + 3.0 * column_ids.astype(jnp.float32) / VOCAB) / math.sqrt(D)
    values = jnp.clip(jax.random.normal(base_key, (D, VOCAB), jnp.float32), -6.0, 6.0) * rising
    strengths = (120.0, 170.0, 230.0)
    for anchor in range(3):
        level = strengths[anchor] / (math.sqrt(2.0 / math.pi) * D)
        column = jnp.sign(directions[anchor]) * level
        lowered = jnp.where(feature_ids % 80 == 0, 0.0, column)
        paired = (columns_at[anchor] + VOCAB // 2) % VOCAB
        values = jnp.where(column_ids == columns_at[anchor], column[:, None], values)
        values = jnp.where(column_ids == paired, lowered[:, None], values)
    return values.astype(jnp.bfloat16)


def touch_ends(entries, key, low, largest):
    index_at = [jax.random.randint(jax.random.fold_in(key, axis), (), 0, length) for axis, length in enumerate(entries.shape)]
    widest = entries.shape.index(max(entries.shape))
    next_to = index_at[:widest] + [(index_at[widest] + 1) % entries.shape[widest]] + index_at[widest + 1:]
    return entries.at[tuple(index_at)].set(low).at[tuple(next_to)].set(largest)


def cumulative_ranks(count, slope):
    portions = [(1 << 20) // math.isqrt(standing ** slope) + 1 for standing in range(1, count + 1)]
    deviation = 1 + sum(portions) // (1 << 30)
    return np.cumsum(np.array([max(1, weight // deviation) for weight in portions]))


def skewed_ids(stream_key, dims, count, skew):
    table = cumulative_ranks(count, skew)
    lot = jax.random.randint(jax.random.fold_in(stream_key, 1), dims, 0, int(table[count - 1]))
    rank = jnp.searchsorted(jnp.asarray(table, jnp.int32), lot, side="right")
    return jax.random.permutation(jax.random.fold_in(stream_key, 2), count)[rank].astype(jnp.int32)


def setup_inputs(seed: int = 0) -> dict:
    seeds = jax.random.split(jax.random.key(seed), 7)
    return {
        "hidden_rows": draw_hidden_rows(jax.random.fold_in(seeds[6], 71), 0),
        "norm_gain": jnp.clip(1.0 + 0.1 * jax.random.normal(seeds[1], (D,), jnp.float32), 0.5, 1.5),
        "head_weight": draw_head_weight(jax.random.fold_in(seeds[6], 71), 0),
        "targets": touch_ends(skewed_ids(seeds[3], (ROWS,), VOCAB, 2), jax.random.fold_in(seeds[3], 3), 0, VOCAB - 1).astype(jnp.int32),
        "exit_layer": touch_ends(jax.random.randint(seeds[4], (SECTIONS,), 0, LAYERS), jax.random.fold_in(seeds[4], 1), 0, LAYERS - 1).astype(jnp.int32),
        "numerators": touch_ends(jax.random.randint(seeds[5], (LAYERS,), 1, 17), jax.random.fold_in(seeds[5], 1), 1, 16).astype(jnp.int32),
    }


EPS = 1e-05

def section_weights(exit_layer, numerators):
    picked = numerators[exit_layer].astype(jnp.float32)
    return picked / jnp.sum(picked)

def reference(hidden_rows, norm_gain, head_weight, targets, exit_layer, numerators):
    weights = section_weights(exit_layer, numerators)
    row_weight = jnp.repeat(weights, ROWS // SECTIONS)
    values = hidden_rows.astype(jnp.float32)
    inverse_rms = lax.rsqrt(lax.optimization_barrier(jnp.mean(values * values, axis=1, keepdims=True)) + EPS)
    normed = (values * inverse_rms * norm_gain[None, :]).astype(jnp.bfloat16)
    logits = jnp.dot(normed, head_weight, preferred_element_type=jnp.float32)
    row_max = lax.optimization_barrier(jnp.max(logits, axis=1, keepdims=True))
    log_total = row_max + jnp.log(lax.optimization_barrier(jnp.sum(jnp.exp(logits - row_max), axis=1, keepdims=True)))
    onehot = jnp.arange(VOCAB, dtype=jnp.int32)[None, :] == targets[:, None]
    picked = lax.optimization_barrier(jnp.sum(jnp.where(onehot, logits, 0.0), axis=1))
    total_loss = jnp.sum(row_weight * (log_total[:, 0] - picked))
    dlogit = (row_weight[:, None] * (jnp.exp(logits - log_total) - onehot.astype(jnp.float32))).astype(jnp.bfloat16)
    head_grad = lax.dot_general(normed, dlogit, (((0,), (0,)), ((), ())), preferred_element_type=jnp.float32).astype(jnp.bfloat16)
    dnormed = lax.dot_general(dlogit, head_weight, (((1,), (1,)), ((), ())), preferred_element_type=jnp.float32)
    gained = dnormed * norm_gain[None, :]
    gain_grad = lax.optimization_barrier(jnp.sum(dnormed * values * inverse_rms, axis=0))
    inner_mean = lax.optimization_barrier(jnp.mean(gained * values, axis=1, keepdims=True))
    hidden_grad = (inverse_rms * gained - values * (inverse_rms * inverse_rms * inverse_rms) * inner_mean).astype(jnp.bfloat16)
    return (hidden_grad, gain_grad, head_grad, total_loss)
```

```python
import jax
import jax.numpy as jnp
from jax import lax
from jax.sharding import PartitionSpec as P

EPS = 1e-05
SIDE = 4
F32 = jnp.float32
BF16 = jnp.bfloat16


def over_section(x, step):
    return lax.ppermute(x, "section", [(i, (i + step) % SIDE) for i in range(SIDE)])


def over_vocab(x, dx=0, dz=0, dc=0):
    pairs = []
    for px in range(SIDE):
        for pz in range(SIDE):
            for pc in range(2):
                to = (((px + dx) % SIDE) * SIDE + (pz + dz) % SIDE) * 2 + (pc ^ dc)
                pairs.append(((px * SIDE + pz) * 2 + pc, to))
    return lax.ppermute(x, "vocab", pairs)


def along_x(x):
    return [x, over_vocab(x, dx=-1), over_vocab(x, dx=2), over_vocab(x, dx=1)]


def encode(x):
    largest = jnp.max(jnp.abs(x), axis=-1, keepdims=True)
    power = jnp.clip(jnp.floor(jnp.log2(jnp.maximum(largest, 1e-30))) + 1.0, -100.0, 100.0)
    codes = jnp.clip(jnp.round(x * jnp.exp2(15.0 - power)), -32767.0, 32767.0)
    tail = jnp.broadcast_to(power, (*x.shape[:-1], 128))
    return jnp.concatenate([codes, tail], axis=-1).astype(jnp.int16)


def decode(message):
    width = message.shape[-1] - 128
    power = message[..., width : width + 1].astype(F32)
    return message[..., :width].astype(F32) * jnp.exp2(power - 15.0)


def section_weights(exit_layer, numerators):
    layers = numerators.shape[0]
    matches = exit_layer[:, None] == jnp.arange(layers, dtype=jnp.int32)[None, :]
    picked = jnp.sum(jnp.where(matches, numerators[None, :], 0), axis=1).astype(F32)
    return picked / jnp.sum(picked)


def reduce_logits(partial):
    half = partial.shape[1] // 2
    up = over_section(encode(partial[2, :half]), 1)
    down = over_section(encode(partial[2, half:]), -1)
    first = jnp.concatenate([partial[1, :half] + decode(up), partial[1, half:]], axis=0)
    last = jnp.concatenate([partial[3, :half], partial[3, half:] + decode(down)], axis=0)
    from_below = over_section(encode(first), 1)
    from_above = over_section(encode(last), -1)
    return partial[0] + (decode(from_below) + decode(from_above))


def gather_sections(own):
    half = own.shape[0] // 2
    below = over_section(own, 1)
    above = over_section(own, -1)
    far_first = over_section(below[:half], 1)
    far_last = over_section(above[half:], -1)
    return jnp.stack([own, above, jnp.concatenate([far_first, far_last], axis=0), below])


def combine(stats):
    top = stats[0][0]
    for other in stats[1:]:
        top = jnp.maximum(top, other[0])
    totals = [s[1] * jnp.exp(s[0] - top) for s in stats]
    picks = [s[2] for s in stats]
    if len(stats) == 2:
        return top, totals[0] + totals[1], picks[0] + picks[1]
    return (
        top,
        (totals[0] + totals[2]) + (totals[1] + totals[3]),
        (picks[0] + picks[2]) + (picks[1] + picks[3]),
    )


def local(hidden_rows, norm_gain, head_weight, targets, exit_layer, numerators):
    section = lax.axis_index("section")
    piece = lax.axis_index("vocab")
    own_rows, width = hidden_rows.shape
    depth, vocab_shard = head_weight.shape
    other_head = over_vocab(head_weight, dc=1)

    values = hidden_rows.astype(F32)
    inverse_rms = lax.rsqrt(jnp.mean(values * values, axis=1, keepdims=True) + EPS)
    normed = (values * inverse_rms * norm_gain[None, :]).astype(BF16)
    lane = jnp.arange(128, dtype=jnp.int32)[None, :]
    digits = jnp.where(lane == 0, targets[:, None] // 256, jnp.where(lane == 1, targets[:, None] % 256, 0))
    digits = digits.astype(BF16)

    def block_of(step):
        at = lax.rem(section + step, SIDE) * depth
        return jnp.concatenate([lax.dynamic_slice(normed, (0, at), (own_rows, depth)), digits], axis=1)

    own = jnp.stack(
        [block_of(0), over_section(block_of(3), -1), over_section(block_of(2), 2), over_section(block_of(1), 1)]
    )
    near = jnp.stack(along_x(own))
    z_up, z_down = over_vocab(own, dz=-1), over_vocab(own, dz=1)
    sides = jnp.stack(along_x(jnp.stack([z_up, z_down])))
    far = over_vocab(near, dz=2)

    def with_other_core(mine):
        both = jnp.stack([mine, over_vocab(mine, dc=1)])
        return jnp.transpose(both, (3, 2, 0, 1, 4, 5))

    chunks = [with_other_core(near[:, None]), with_other_core(sides), with_other_core(far[:, None])]
    logits, wanted, columns = [], [], []
    base = piece * vocab_shard
    column_ids = base + jnp.arange(vocab_shard, dtype=jnp.int32)
    for chunk in chunks:
        rows = chunk.reshape(-1, depth + 128)
        block = rows[:, :depth]
        columns.append(chunk[..., :depth])
        partial = jnp.dot(block, head_weight, preferred_element_type=F32)
        own_part = partial.reshape(SIDE, -1, vocab_shard)
        logits.append(reduce_logits(own_part))
        digit = chunk[0].reshape(-1, depth + 128)[:, depth : depth + 2].astype(jnp.int32)
        wanted.append(digit[:, 0] * 256 + digit[:, 1])

    stats = []
    for rows, want in zip(logits, wanted):
        top = jnp.max(rows, axis=1)
        total = jnp.sum(jnp.exp(rows - top[:, None]), axis=1)
        pick = jnp.sum(jnp.where(column_ids[None, :] == want[:, None], rows, 0.0), axis=1)
        stats.append(jnp.stack([top, total, pick]))
    quarter = 2 * SIDE * own_rows
    joined = jnp.concatenate(
        [stats[0], stats[1][:, :quarter], stats[2], stats[1][:, quarter:]], axis=1
    ).reshape(3, SIDE * 2, SIDE * own_rows)

    def parts(x):
        return x[0], x[1], x[2]

    def swap_core(x):
        return x.reshape(3, SIDE, 2, SIDE * own_rows)[:, :, ::-1].reshape(x.shape)

    joined = jnp.stack(combine([parts(joined), parts(swap_core(over_vocab(joined, dc=1)))]))
    got = along_x(joined)
    got = [parts(jnp.roll(g, d * own_rows, axis=2)) for d, g in enumerate(got)]
    joined = jnp.stack(combine(got))
    got = [joined, over_vocab(joined, dz=-1), over_vocab(joined, dz=2), over_vocab(joined, dz=1)]
    got = [parts(jnp.roll(g, d * 2, axis=1)) for d, g in enumerate(got)]
    top, total, pick = combine(got)
    log_total = top + jnp.log(total)

    weights = section_weights(exit_layer, numerators)
    mine = jnp.sum(jnp.where(jnp.arange(SIDE) == section, weights, 0.0))
    x_at, z_at, c_at = piece // 8, (piece // 2) % SIDE, piece % 2
    loss_rows = (log_total - pick).reshape(SIDE, 2, SIDE, own_rows)
    loss_rows = jnp.where(c_at == 1, loss_rows[:, ::-1], loss_rows)
    loss_rows = jnp.roll(jnp.roll(loss_rows, z_at, axis=0), x_at, axis=2)
    part = jnp.broadcast_to(mine * jnp.sum(loss_rows), (8, 128))
    loss = (part + over_section(part, 2)) + (over_section(part, 1) + over_section(part, -1))
    total_loss = loss[0, 0]

    by_dz = log_total.reshape(SIDE, quarter)
    row_totals = [by_dz[0], jnp.concatenate([by_dz[1], by_dz[3]]), by_dz[2]]
    grads = []
    for rows, want, lt in zip(logits, wanted, row_totals):
        onehot = (column_ids[None, :] == want[:, None]).astype(F32)
        grads.append((mine * (jnp.exp(rows - lt[:, None]) - onehot)).astype(BF16))

    gathered, sums = {}, {}
    for name in (2, 1, 0):
        whole = gather_sections(grads[name])
        gathered[name] = whole
        split = whole.reshape(SIDE, -1, 2, SIDE * own_rows, vocab_shard)
        mine_rows, their_rows = split[:, :, 0], split[:, :, 1]
        got = over_vocab(their_rows, dc=1)
        n = split.shape[1]
        dims = (((1,), (1,)), ((), ()))
        out = lax.dot_general(
            mine_rows.reshape(-1, vocab_shard), head_weight, dims, preferred_element_type=F32
        ) + lax.dot_general(got.reshape(-1, vocab_shard), other_head, dims, preferred_element_type=F32)
        sums[name] = out.reshape(SIDE, n, SIDE, own_rows, depth)
    to_far = over_vocab(sums[2][:, 0].astype(BF16), dz=2)
    to_up = over_vocab(sums[1][:, 0].astype(BF16), dz=1)
    to_down = over_vocab(sums[1][:, 1].astype(BF16), dz=-1)
    reduced = (sums[0][:, 0] + to_far.astype(F32)) + (to_up.astype(F32) + to_down.astype(F32))
    sent = reduced.astype(BF16)
    x_far = over_vocab(sent[:, 2], dx=2)
    x_up = over_vocab(sent[:, 1], dx=1)
    x_down = over_vocab(sent[:, 3], dx=-1)
    block = (reduced[:, 0] + x_far.astype(F32)) + (x_up.astype(F32) + x_down.astype(F32))
    got = [block[0], over_section(block[3], -1), over_section(block[2], 2), over_section(block[1], 1)]
    in_order = jnp.concatenate(got, axis=1)
    dnormed = jnp.roll(in_order, section * depth, axis=1)

    head_grad = sum(
        lax.dot_general(
            c.reshape(-1, depth), gathered[i].reshape(-1, vocab_shard), (((0,), (0,)), ((), ())),
            preferred_element_type=F32,
        )
        for i, c in enumerate(columns)
    ).astype(BF16)

    gained = dnormed * norm_gain[None, :]
    inner_mean = jnp.mean(gained * values, axis=1, keepdims=True)
    hidden_grad = (
        inverse_rms * gained - values * (inverse_rms * inverse_rms * inverse_rms) * inner_mean
    ).astype(BF16)
    gain = jnp.sum(dnormed * values * inverse_rms, axis=0).reshape(64, 128)
    gain = gain + over_vocab(gain, dc=1)
    gain = (gain + over_vocab(gain, dx=2)) + (over_vocab(gain, dx=1) + over_vocab(gain, dx=-1))
    gain = (gain + over_vocab(gain, dz=2)) + (over_vocab(gain, dz=1) + over_vocab(gain, dz=-1))
    gain = (gain + over_section(gain, 2)) + (over_section(gain, 1) + over_section(gain, -1))
    return (hidden_grad, gain.reshape(width), head_grad, total_loss)


def solution(mesh):
    return jax.shard_map(
        local,
        mesh=mesh,
        in_specs=(
            P(("section", "vocab"), None),
            P(),
            P("section", "vocab"),
            P(("section", "vocab")),
            P(),
            P(),
        ),
        out_specs=(P(("section", "vocab"), None), P(), P("section", "vocab"), P()),
        check_vma=False,
    )
```

```python
import functools
import jax
import jax.numpy as jnp
from jax import lax
from jax.experimental import pallas as pl
from jax.experimental.pallas import tpu as pltpu
from jax.sharding import PartitionSpec as P

EPS = 1e-05
SIDE = 4
TAIL = 128
TILE = 256
F32 = jnp.float32
BF16 = jnp.bfloat16
ANY = pl.BlockSpec(memory_space=pl.ANY)
VMEM = pl.BlockSpec(memory_space=pltpu.VMEM)
SMEM = pl.BlockSpec(memory_space=pltpu.SMEM)
PARAMS = pltpu.CompilerParams(vmem_limit_bytes=22 * 2**20)


def over_section(x, step):
    return lax.ppermute(x, "section", [(i, (i + step) % SIDE) for i in range(SIDE)])


def over_vocab(x, dx=0, dz=0, dc=0):
    pairs = []
    for px in range(SIDE):
        for pz in range(SIDE):
            for pc in range(2):
                to = (((px + dx) % SIDE) * SIDE + (pz + dz) % SIDE) * 2 + (pc ^ dc)
                pairs.append(((px * SIDE + pz) * 2 + pc, to))
    return lax.ppermute(x, "vocab", pairs)


def shape(*dims, dtype=F32):
    return jax.ShapeDtypeStruct(dims, dtype)


def cost(flops, moved):
    return pl.CostEstimate(flops=flops, bytes_accessed=moved, transcendentals=0)


def in_vmem(x):
    return pltpu.with_memory_space_constraint(x, pltpu.VMEM)


def in_hbm(x):
    return pltpu.with_memory_space_constraint(x, pltpu.HBM)


def launch(kernel, operands, after=(), *, in_specs, scratch_shapes=(), name, **options):
    used, ignored = len(operands), len(after)

    def body(*refs):
        kernel(*refs[:used], *refs[used + ignored :])

    return pl.pallas_call(
        body,
        in_specs=[*in_specs, *[ANY] * ignored],
        scratch_shapes=list(scratch_shapes),
        compiler_params=PARAMS,
        name=name,
        **options,
    )(*operands, *after)


def encode(x, message, at):
    rows, width = x.shape
    largest = jnp.max(jnp.abs(x), axis=1, keepdims=True)
    power = jnp.clip(jnp.floor(jnp.log2(jnp.maximum(largest, 1e-30))) + 1.0, -100.0, 100.0)
    codes = jnp.clip(jnp.round(x * jnp.exp2(15.0 - power)), -32767.0, 32767.0)
    message[pl.ds(at, rows), :width] = codes.astype(jnp.int32).astype(jnp.int16)
    tail = jnp.broadcast_to(power, (rows, TAIL)).astype(jnp.int32)
    message[pl.ds(at, rows), width:] = tail.astype(jnp.int16)


def decode(message, at, rows):
    width = message.shape[1] - TAIL
    power = message[pl.ds(at, rows), width:].astype(jnp.int32).astype(F32)[:, :1]
    codes = message[pl.ds(at, rows), :width].astype(jnp.int32).astype(F32)
    return codes * jnp.exp2(power - 15.0)


def hold_kernel(head, held, sem):
    copy = pltpu.make_async_copy(head, held, sem)
    copy.start()
    copy.wait()


def hold(head, after=()):
    return launch(
        hold_kernel,
        (in_hbm(head),),
        after,
        out_shape=pltpu.VMEM(head.shape, head.dtype),
        in_specs=[ANY],
        out_specs=VMEM,
        scratch_shapes=[pltpu.SemaphoreType.DMA(())],
        cost_estimate=cost(0, 2 * head.size),
        name="hold_head",
    )


def normalise_kernel(place, hidden, gain, targets, *blocks):
    rows, width = hidden.shape
    depth = width // SIDE
    values = hidden[...].astype(F32)
    inverse = lax.rsqrt(jnp.mean(values * values, axis=1, keepdims=True) + EPS)
    lane = lax.broadcasted_iota(jnp.int32, (rows, TAIL), 1)
    row = lax.broadcasted_iota(jnp.int32, (rows, TAIL), 0)
    digits = jnp.zeros((rows, TAIL), jnp.int32)
    for i in range(rows):
        high = targets[i] // 256
        low = targets[i] - high * 256
        digits = jnp.where(row == i, jnp.where(lane == 0, high, jnp.where(lane == 1, low, 0)), digits)
    digits = digits.astype(F32).astype(BF16)
    for step in range(SIDE):
        at = pl.multiple_of(lax.rem(place[0] + step, SIDE) * depth, depth)
        cut = hidden[:, pl.ds(at, depth)].astype(F32) * inverse * gain[:, pl.ds(at, depth)]
        blocks[step][:, :depth] = cut.astype(BF16)
        blocks[step][:, depth:] = digits


def normalise(place, hidden, gain, targets, after=()):
    rows, width = hidden.shape
    return launch(
        normalise_kernel,
        (place, hidden, gain, targets,),
        after,
        out_shape=[shape(rows, width // SIDE + TAIL, dtype=BF16)] * SIDE,
        in_specs=[SMEM, VMEM, VMEM, SMEM],
        out_specs=[VMEM] * SIDE,
        cost_estimate=cost(10 * rows * width, 8 * rows * width),
        name="normalise",
    )


def logits_kernel(offsets, count, *refs):
    pieces, head, refs = refs[:count], refs[count], refs[count + 1 :]
    depth, columns = head.shape
    outs, (rows, sems) = refs[:2], refs[-2:]
    per = rows.shape[1]
    step = pl.program_id(0)

    @pl.when(step == 0)
    def _():
        copies = []
        for i, ds in enumerate(offsets):
            at = 0
            for piece in pieces:
                span = piece.shape[1]
                to = rows.at[i, pl.ds(at, span), :]
                sem = sems.at[len(copies)]
                copies.append(pltpu.make_async_copy(piece.at[ds, :, pl.ds(0, depth)], to, sem))
                at += span
        for copy in copies:
            copy.start()
        for copy in copies:
            copy.wait()

    cut = pl.ds(pl.multiple_of(step * TILE, TILE), TILE)
    part = jnp.dot(rows[...].reshape(-1, depth), head[:, cut], preferred_element_type=F32)
    if offsets != (2,):
        for i in range(len(offsets)):
            outs[i][...] = part[i * per : (i + 1) * per]
        return
    far = refs[2]
    far[:, cut] = part

    @pl.when(step == pl.num_programs(0) - 1)
    def _():
        half = per // 2
        for at in range(0, half, 32):
            encode(far[pl.ds(at, 32), :], outs[0], at)
            encode(far[pl.ds(half + at, 32), :], outs[1], at)


def logits_of(offsets, pieces, head, after=()):
    depth, columns = head.shape
    count, per = len(offsets), sum(p.shape[1] for p in pieces)
    if offsets == (2,):
        outs = [shape(per // 2, columns + TAIL, dtype=jnp.int16)] * 2
        specs = [pl.BlockSpec((per // 2, columns + TAIL), lambda j: (0, 0))] * 2
        scratch = [pltpu.VMEM((per, columns), F32)]
    else:
        outs = [shape(per, columns)] * count
        specs = [pl.BlockSpec((per, TILE), lambda j: (0, j))] * count
        scratch = []
    scratch += [pltpu.VMEM((count, per, depth), BF16), pltpu.SemaphoreType.DMA((count * len(pieces),))]
    kernel = functools.partial(logits_kernel, offsets, len(pieces))
    if count == 1 and offsets != (2,):
        def kernel(*refs):
            at = len(pieces) + 1
            logits_kernel(offsets, len(pieces), *refs[: at + 1], None, *refs[at + 1 :])

    return launch(
        kernel,
        (*pieces, in_vmem(head)),
        after,
        grid=(columns // TILE,),
        out_shape=outs,
        in_specs=[ANY] * len(pieces) + [VMEM],
        out_specs=specs,
        scratch_shapes=scratch,
        cost_estimate=cost(0, 2 * depth * columns + 4 * count * per * columns),
        name="partial_logits",
    )


def pass_on_kernel(first, last, up, down, to_first, to_last):
    per = first.shape[0]
    half = per // 2
    for at in range(0, half, 32):
        encode(first[pl.ds(at, 32), :] + decode(up, at, 32), to_first, at)
        encode(last[pl.ds(at, 32), :], to_last, at)
        encode(first[pl.ds(half + at, 32), :], to_first, half + at)
        encode(last[pl.ds(half + at, 32), :] + decode(down, at, 32), to_last, half + at)


def pass_on(first, last, up, down, after=()):
    per, columns = first.shape
    return launch(
        pass_on_kernel,
        (first, last, up, down,),
        after,
        out_shape=[shape(per, columns + TAIL, dtype=jnp.int16)] * 2,
        in_specs=[VMEM] * 4,
        out_specs=[VMEM] * 2,
        cost_estimate=cost(20 * per * columns, 14 * per * columns),
        name="pass_on",
    )


def onehot_of(place, digits, columns):
    want = digits[:, :1].astype(F32) * 256.0 + digits[:, 1:2].astype(F32)
    want = want.astype(jnp.int32) - place[4]
    return lax.broadcasted_iota(jnp.int32, (digits.shape[0], columns), 1) == want


def own_logits_kernel(count, place, own, below, above, *refs):
    digits, (exps, stats) = refs[: 2 * count], refs[2 * count :]
    per, columns = own.shape
    at = 0
    for digit in digits:
        span = digit.shape[1]
        lane = lax.broadcasted_iota(jnp.int32, (span, TAIL), 1)
        x = own[pl.ds(at, span), :] + (decode(below, at, span) + decode(above, at, span))
        top = jnp.max(x, axis=1, keepdims=True)
        exp = jnp.exp(x - top)
        exps[at // (per // 2), pl.ds(at % (per // 2), span), :] = exp.astype(BF16)
        total = jnp.sum(exp, axis=1, keepdims=True)
        pick = jnp.sum(jnp.where(onehot_of(place, digit[0], columns), x, 0.0), axis=1, keepdims=True)
        stats[pl.ds(at, span), :] = jnp.where(lane == 0, top, jnp.where(lane == 1, total, pick))
        at += span


def digit_specs(pieces):
    at = pieces[0].shape[2] // TAIL - 1
    return [pl.BlockSpec((1, p.shape[1], TAIL), lambda j: (0, 0, at)) for p in pieces]


def own_logits(place, own, below, above, mine, theirs, after=()):
    per, columns = own.shape
    full = pl.BlockSpec((per, columns), lambda j: (0, 0))
    coded = pl.BlockSpec((per, columns + TAIL), lambda j: (0, 0))
    return launch(
        functools.partial(own_logits_kernel, len(mine)),
        (place, own, below, above, *mine, *theirs),
        after,
        grid=(1,),
        out_shape=[shape(2, per // 2, columns, dtype=BF16), shape(per, TAIL)],
        in_specs=[SMEM, full, coded, coded] + digit_specs([*mine, *theirs]),
        out_specs=[pl.BlockSpec((2, per // 2, columns), lambda j: (0, 0, 0)), pl.BlockSpec((per, TAIL), lambda j: (0, 0))],
        cost_estimate=cost(20 * per * columns, 12 * per * columns),
        name="own_logits",
    )


def at_owner(place, dz, dc, dx, size):
    z = lax.rem(place[2] + dz, SIDE)
    x = lax.rem(place[1] + dx, SIDE)
    c = lax.rem(place[3] + dc, 2)
    return pl.multiple_of(((z * 2 + c) * SIDE + x) * size, size)


def walk(groups, size):
    for g, offsets in enumerate(groups):
        at = 0
        for dc in range(2):
            for dz in offsets:
                for dx in range(SIDE):
                    yield g, at, dz, dc, dx
                    at += size


def pack_kernel(groups, size, place, *refs):
    stats, (message, ordered) = refs[: len(groups)], refs[len(groups) :]
    for g, at, dz, dc, dx in walk(groups, size):
        ordered[pl.ds(at_owner(place, dz, dc, dx, size), size), :] = stats[g][pl.ds(at, size), :]
    message[...] = jnp.transpose(ordered[...])[:8]


def pack(place, stats, groups, size, after=()):
    rows = sum(s.shape[0] for s in stats)
    return launch(
        functools.partial(pack_kernel, groups, size),
        (place, *stats,),
        after,
        out_shape=shape(8, rows),
        in_specs=[SMEM] + [VMEM] * len(stats),
        out_specs=VMEM,
        scratch_shapes=[pltpu.VMEM((rows, TAIL), F32)],
        cost_estimate=cost(rows * TAIL, rows * TAIL * 4),
        name="pack_statistics",
    )


def merged(stats):
    tops = [x[:1] for x in stats]
    top = functools.reduce(jnp.maximum, tops)
    totals = [x[1:2] * jnp.exp(t - top) for x, t in zip(stats, tops)]
    picks = [x[2:3] for x in stats]
    if len(stats) == 4:
        totals, picks = ([x[0] + x[2], x[1] + x[3]] for x in (totals, picks))
    return top, totals[0] + totals[1], picks[0] + picks[1]


def merge_kernel(*refs):
    top, total, pick = merged([ref[...] for ref in refs[:-1]])
    row = lax.broadcasted_iota(jnp.int32, refs[-1].shape, 0)
    refs[-1][...] = jnp.where(row == 0, top, jnp.where(row == 1, total, pick))


def merge(stats, after=()):
    return launch(
        merge_kernel,
        (*stats,),
        after,
        out_shape=shape(*stats[0].shape),
        in_specs=[VMEM] * len(stats),
        out_specs=VMEM,
        cost_estimate=cost(64 * stats[0].size, 32 * stats[0].size),
        name="merge_statistics",
    )


def combine_kernel(offsets, size, count, place, weight, *refs):
    parts, (stats, message, ordered, scale) = refs[:count], refs[count:]
    top, total, pick = merged([ref[...] for ref in parts])
    log_total = top + jnp.log(total)
    loss = weight[0] * jnp.sum(log_total - pick, axis=1, keepdims=True)
    ordered[...] = jnp.transpose(jnp.broadcast_to(log_total, (TAIL, log_total.shape[1])))
    for _, at, dz, dc, dx in walk((offsets,), size):
        rows = ordered[pl.ds(at_owner(place, dz, dc, dx, size), size), :]
        scale[pl.ds(at, size), :] = weight[0] * jnp.exp(stats[pl.ds(at, size), :1] - rows)
    scales = jnp.transpose(scale[...])[:8]
    row = lax.broadcasted_iota(jnp.int32, scales.shape, 0)
    message[...] = jnp.where(row == 0, scales, jnp.where(row == 1, weight[0], loss))


def combine(place, weight, parts, stats, offsets, size, after=()):
    rows = stats.shape[0]
    return launch(
        functools.partial(combine_kernel, offsets, size, len(parts)),
        (place, weight, *parts, stats),
        after,
        out_shape=shape(8, rows),
        in_specs=[SMEM, SMEM] + [VMEM] * (len(parts) + 1),
        out_specs=VMEM,
        scratch_shapes=[pltpu.VMEM((rows, TAIL), F32)] * 2,
        cost_estimate=cost(rows * TAIL, rows * TAIL * 4),
        name="combine_statistics",
    )


def halves_kernel(below, above, first, last):
    first[...] = below[0]
    last[...] = above[1]


def halves(below, above, after=()):
    out = shape(*below.shape[1:], dtype=below.dtype)
    return launch(
        halves_kernel,
        (below, above),
        after,
        out_shape=[out] * 2,
        in_specs=[VMEM] * 2,
        out_specs=[VMEM] * 2,
        cost_estimate=cost(0, 4 * below.size),
        name="halves",
    )


def dlogit_kernel(dc, place, *refs):
    scales, (own, above, far, below), digits, out = refs[:SIDE], refs[SIDE : 2 * SIDE], refs[2 * SIDE : -1], refs[-1]
    half, columns = far.shape
    for ds in range(SIDE):
        scale = jnp.transpose(jnp.broadcast_to(scales[ds][:1], (TAIL, 2 * half)))
        weight = scales[ds][1:2, :1]
        at = 0
        for digit in digits:
            span = digit.shape[1]
            exp = far[pl.ds(at, span), :] if ds == 2 else (own, above, None, below)[ds][0, pl.ds(at, span), :]
            hit = onehot_of(place, digit[ds], columns)
            factor = scale[dc * half + at : dc * half + at + span, :1]
            grad = exp.astype(F32) * factor - jnp.where(hit, weight, 0.0)
            out[ds, pl.ds(at, span), :] = grad.astype(BF16)
            at += span


def dlogit_of(dc, place, scales, own, above, far, below, pieces, after=()):
    half, columns = far.shape
    at = pieces[0].shape[2] // TAIL - 1
    one = pl.BlockSpec((1, half, columns), lambda j: (dc, 0, 0))
    return launch(
        functools.partial(dlogit_kernel, dc),
        (place, *scales, own, above, far, below, *pieces),
        after,
        grid=(1,),
        out_shape=shape(SIDE, half, columns, dtype=BF16),
        in_specs=[SMEM]
        + [pl.BlockSpec(scales[0].shape, lambda j: (0, 0))] * SIDE
        + [one, one, pl.BlockSpec((half, columns), lambda j: (0, 0)), one]
        + [pl.BlockSpec((SIDE, p.shape[1], TAIL), lambda j: (0, 0, at)) for p in pieces],
        out_specs=pl.BlockSpec((SIDE, half, columns), lambda j: (0, 0, 0)),
        cost_estimate=cost(40 * half * columns, 16 * half * columns),
        name="dlogit",
    )


def dnormed_kernel(first, count, left, right, head, other, *refs):
    normed, outs, gain = refs[: -1 - count], refs[-1 - count : -1], refs[-1]
    columns = head.shape[1]
    dims = (((1,), (1,)), ((), ()))
    cut = pl.ds(pl.multiple_of(pl.program_id(0) * TILE, TILE), TILE)
    span = outs[0].shape[1]
    rows = pl.ds(first, count * span)
    part = lax.dot_general(left[:, rows, :].reshape(-1, columns), head[cut, :], dims, preferred_element_type=F32)
    part = part + lax.dot_general(
        right[:, rows, :].reshape(-1, columns), other[cut, :], dims, preferred_element_type=F32
    )
    x = jnp.concatenate([n[...] for n in normed], axis=1).reshape(part.shape).astype(F32)
    gain[...] = jnp.sum((part * x).reshape(-1, 8, TILE), axis=0)
    part = part.reshape(SIDE, count, -1, TILE)
    for k in range(count):
        outs[k][...] = part[:, k].astype(outs[k].dtype)


def dnormed_of(first, left, right, head, other, normed, span, dtype, after=()):
    depth, columns = head.shape
    count = sum(n.shape[1] for n in normed) // span
    block = pl.BlockSpec((SIDE, span, TILE), lambda j: (0, 0, j))
    return launch(
        functools.partial(dnormed_kernel, first, count),
        (left, right, in_vmem(head), in_vmem(other), *normed),
        after,
        grid=(depth // TILE,),
        out_shape=[shape(SIDE, span, depth, dtype=dtype)] * count + [shape(8, depth)],
        in_specs=[VMEM] * 4 + [pl.BlockSpec((SIDE, n.shape[1], TILE), lambda j: (0, 0, j)) for n in normed],
        out_specs=[block] * count + [pl.BlockSpec((8, TILE), lambda j: (0, j))],
        cost_estimate=cost(0, 4 * depth * columns),
        name="dnormed",
    )


def head_grad_kernel(count, *refs):
    pieces, (ours, others) = refs[:count], refs[count : count + 2]
    out, token, grads, sems = refs[-4:]
    token[...] = jnp.zeros_like(token)

    @pl.when(pl.program_id(0) == 0)
    def _():
        copies = [(ours, grads.at[:, 0]), (others, grads.at[:, 1])]
        copies = [pltpu.make_async_copy(a, b, sems.at[i]) for i, (a, b) in enumerate(copies)]
        for copy in copies:
            copy.start()
        for copy in copies:
            copy.wait()

    x = jnp.concatenate([piece[...] for piece in pieces], axis=1).reshape(-1, TILE)
    y = grads[...].reshape(x.shape[0], -1)
    out[...] = lax.dot_general(x, y, (((0,), (0,)), ((), ())), preferred_element_type=F32).astype(BF16)


def head_grad_of(pieces, ours, others, depth, start, stop, into=None, after=()):
    columns, rows = ours.shape[2], 2 * SIDE * ours.shape[1]
    inputs = [in_hbm(x) for x in (*pieces, ours, others)]
    specs = [pl.BlockSpec((SIDE, p.shape[1], TILE), lambda j: (0, 0, start + j)) for p in pieces] + [ANY] * 2
    aliases = {}
    if into is not None:
        aliases = {len(inputs): 0}
        inputs.append(in_hbm(into))
        specs.append(ANY)
    return launch(
        functools.partial(head_grad_kernel, len(pieces)),
        (*inputs,),
        after,
        grid=(stop - start,),
        input_output_aliases=aliases,
        out_shape=[shape(depth, columns, dtype=BF16), shape(8, TAIL)],
        in_specs=specs,
        out_specs=[pl.BlockSpec((TILE, columns), lambda j: (start + j, 0)), pl.BlockSpec((8, TAIL), lambda j: (0, 0))],
        scratch_shapes=[pltpu.VMEM((SIDE, 2, *ours.shape[1:]), BF16), pltpu.SemaphoreType.DMA((2,))],
        cost_estimate=cost(2 * rows * (stop - start) * TILE * columns, depth * columns + 4 * rows * depth),
        name="head_grad",
    )


def spread_kernel(near, own, out):
    gain = jnp.sum(near[...] + own[...], axis=0, keepdims=True)
    wide = out.shape[2]
    gain = jnp.concatenate([gain[:, i * wide : (i + 1) * wide] for i in range(out.shape[1])], axis=0)
    out[...] = jnp.broadcast_to(gain, out.shape)


def spread(near, own, after=()):
    rows, depth = near.shape
    return launch(
        spread_kernel,
        (near, own),
        after,
        out_shape=shape(8 * SIDE, rows, depth // rows),
        in_specs=[VMEM] * 2,
        out_specs=VMEM,
        cost_estimate=cost(rows * depth, 4 * 8 * SIDE * depth),
        name="gain_parts",
    )


def to_x_kernel(own, far, up, down, block, *messages):
    total = (own[...] + far[...].astype(F32)) + (up[...].astype(F32) + down[...].astype(F32))
    rows = own.shape[1] // SIDE
    for dx in range(SIDE):
        cut = jnp.concatenate([total[ds, dx * rows : (dx + 1) * rows] for ds in range(SIDE)], axis=0)
        if dx == 0:
            block[...] = cut
        else:
            messages[dx - 1][...] = cut.astype(BF16)


def to_x(own, far, up, down, after=()):
    _, span, depth = own.shape
    return launch(
        to_x_kernel,
        (own, far, up, down),
        after,
        out_shape=[shape(span, depth)] + [shape(span, depth, dtype=BF16)] * 3,
        in_specs=[VMEM] * 4,
        out_specs=[VMEM] * 4,
        cost_estimate=cost(8 * span * depth, 48 * span * depth),
        name="over_x",
    )


def to_y_kernel(place, block, up, far, down, gains, loss, message):
    span, depth = block.shape
    total = (block[...] + far[...].astype(F32)) + (up[...].astype(F32) + down[...].astype(F32))
    gain = jnp.sum(gains[...], axis=0)
    gain = jnp.concatenate([gain[i : i + 1] for i in range(gain.shape[0])], axis=1)
    rows = span // SIDE
    row = lax.broadcasted_iota(jnp.int32, (rows, depth), 0)
    extra = jnp.where(row == 0, gain, jnp.where(row == 1, loss[2:3, :1], 0.0))
    for ds in range(SIDE):
        filled = jnp.concatenate([total[ds * rows : (ds + 1) * rows], extra], axis=0)
        message[lax.rem(place[0] + ds, SIDE)] = filled


def to_y(place, block, up, far, down, gains, loss, after=()):
    span, depth = block.shape
    return launch(
        to_y_kernel,
        (place, block, up, far, down, gains, loss),
        after,
        out_shape=shape(SIDE, 2 * span // SIDE, depth),
        in_specs=[SMEM] + [VMEM] * 6,
        out_specs=VMEM,
        cost_estimate=cost(8 * span * depth, 16 * span * depth),
        name="over_y",
    )


def finish_kernel(hidden, gain, message, out, gain_out, loss_out, dnormed):
    rows, width = hidden.shape
    depth = width // SIDE
    for s in range(SIDE):
        cut = pl.ds(s * depth, depth)
        dnormed[:, cut] = message[s, :rows]
        gain_out[:, cut] = message[s, rows : rows + 1] / gain[:, cut]
    loss = message[:, rows + 1, :TAIL]
    loss_out[...] = jnp.sum(loss, axis=0, keepdims=True)
    values = hidden[...].astype(F32)
    inverse = lax.rsqrt(jnp.mean(values * values, axis=1, keepdims=True) + EPS)
    gained = dnormed[...] * gain[...]
    inner = jnp.mean(gained * values, axis=1, keepdims=True)
    out[...] = (inverse * gained - values * (inverse * inverse * inverse) * inner).astype(BF16)


def finish(hidden, gain, message, after=()):
    rows, width = hidden.shape
    return launch(
        finish_kernel,
        (hidden, gain, message),
        after,
        out_shape=[shape(rows, width, dtype=BF16), shape(1, width), shape(1, TAIL)],
        in_specs=[VMEM] * 3,
        out_specs=[VMEM] * 3,
        scratch_shapes=[pltpu.VMEM((rows, width), F32)],
        cost_estimate=cost(12 * rows * width, 16 * rows * width),
        name="finish",
    )


def section_weights(exit_layer, numerators):
    layers = numerators.shape[0]
    matches = exit_layer[:, None] == jnp.arange(layers, dtype=jnp.int32)[None, :]
    picked = jnp.sum(jnp.where(matches, numerators[None, :], 0), axis=1).astype(F32)
    return picked / jnp.sum(picked)


def local(hidden_rows, norm_gain, head_weight, targets, exit_layer, numerators):
    section, piece = lax.axis_index("section"), lax.axis_index("vocab")
    own_rows, width = hidden_rows.shape
    depth, columns = head_weight.shape
    place = jnp.stack([section, piece // 8, (piece // 2) % SIDE, piece % 2, piece * columns]).astype(jnp.int32)
    gain_row = norm_gain.reshape(1, width)
    weights = section_weights(exit_layer, numerators)
    weight = jnp.sum(jnp.where(jnp.arange(SIDE) == section, weights, 0.0)).reshape(1)

    cuts = normalise(place, hidden_rows, gain_row, targets, (weight,))
    own = jnp.stack([cuts[0], over_section(cuts[3], -1), over_section(cuts[2], 2), over_section(cuts[1], 1)])
    def along_x(x):
        return [x, over_vocab(x, dx=-1), over_vocab(x, dx=2), over_vocab(x, dx=1)]

    pair = jnp.stack([over_vocab(own, dz=-1), over_vocab(own, dz=1)], axis=1)
    mine = [jnp.concatenate(along_x(own), axis=1)]
    mine.append(jnp.stack(along_x(pair), axis=2).reshape(SIDE, -1, own.shape[2]))
    mine.append(over_vocab(mine[0], dz=2))
    theirs = [over_vocab(m, dc=1) for m in mine]
    pieces = (*mine, *theirs)
    groups = ((0,), (1, 3), (2,))
    everything = (sum(groups, ()),)

    held_head = hold(head_weight, (own,))
    up, down = logits_of((2,), pieces, held_head)
    head_ready, _ = lax.optimization_barrier((head_weight, up))
    other_head = over_vocab(head_ready, dc=1)
    first, last = logits_of((1, 3), pieces, held_head, (up,))
    up, down = over_section(up, 1), over_section(down, -1)
    first, last = pass_on(first, last, up, down)
    (kept,) = logits_of((0,), pieces, held_head, (first,))
    held_other = hold(other_head, (kept,))
    below, above = over_section(first, 1), over_section(last, -1)
    exps, stats = own_logits(place, kept, below, above, mine, theirs)

    below, above = over_section(exps, 1), over_section(exps, -1)
    parts = pack(place, [stats], everything, own_rows, (held_other,))
    parts = merge([parts, over_vocab(parts, dc=1)])
    parts = merge(along_x(parts))
    far_first, far_last = halves(below, above, (parts,))
    far_first, far_last = over_section(far_first, 1), over_section(far_last, -1)
    parts = [parts, over_vocab(parts, dz=-1), over_vocab(parts, dz=2), over_vocab(parts, dz=1)]
    scales = combine(place, weight, parts, stats, everything[0], own_rows)
    loss = scales
    scales = [scales, over_section(scales, -1), over_section(scales, 2), over_section(scales, 1)]

    others = dlogit_of(1, place, scales, exps, above, far_last, below, theirs, (far_first,))
    swapped = over_vocab(others, dc=1)
    ours = dlogit_of(0, place, scales, exps, above, far_first, below, mine, (others,))
    span = mine[0].shape[1]
    to_up, to_down, to_far, gain_near = dnormed_of(
        span, ours, swapped, held_head, held_other, mine[1:], span, BF16
    )
    moved = [over_vocab(to_far, dz=2), over_vocab(to_up, dz=1), over_vocab(to_down, dz=-1)]
    kept, gain_own = dnormed_of(0, ours, swapped, held_head, held_other, mine[:1], span, F32, (gain_near,))

    gains = lax.all_to_all(spread(gain_near, gain_own), "vocab", 0, 0)
    tiles = depth // TILE
    grad, token = head_grad_of(pieces, ours, others, depth, 0, tiles // 2, None, (gain_own,))
    block, *cuts = to_x(kept, *moved, (token,))
    cuts = [over_vocab(cuts[0], dx=1), over_vocab(cuts[1], dx=2), over_vocab(cuts[2], dx=-1)]
    grad, token = head_grad_of(pieces, ours, others, depth, tiles // 2, 3 * tiles // 4, grad, (block,))
    message = to_y(place, block, *cuts, gains, loss, (token,))
    got = lax.all_to_all(message, "section", 0, 0)
    head_grad, token = head_grad_of(pieces, ours, others, depth, 3 * tiles // 4, tiles, grad, (message,))
    hidden_grad, gain_grad, total_loss = finish(hidden_rows, gain_row, got, (token,))
    return (hidden_grad, gain_grad.reshape(width), head_grad, total_loss[0, 0])


def solution(mesh):
    return jax.shard_map(
        local,
        mesh=mesh,
        in_specs=(
            P(("section", "vocab"), None),
            P(),
            P("section", "vocab"),
            P(("section", "vocab")),
            P(),
            P(),
        ),
        out_specs=(P(("section", "vocab"), None), P(), P("section", "vocab"), P()),
        check_vma=False,
    )
```

```python
import functools
import jax
import jax.numpy as jnp
from jax import lax
from jax.experimental import pallas as pl
from jax.experimental.pallas import tpu as pltpu
from jax.sharding import PartitionSpec as P

EPS = 1e-05
SIDE = 4
TAIL = 128
TILE = 256
F32 = jnp.float32
BF16 = jnp.bfloat16
ANY = pl.BlockSpec(memory_space=pl.ANY)
VMEM = pl.BlockSpec(memory_space=pltpu.VMEM)
SMEM = pl.BlockSpec(memory_space=pltpu.SMEM)
PARAMS = pltpu.CompilerParams(vmem_limit_bytes=22 * 2**20)


def over_section(x, step):
    return lax.ppermute(x, "section", [(i, (i + step) % SIDE) for i in range(SIDE)])


def over_vocab(x, dx=0, dz=0, dc=0):
    pairs = []
    for px in range(SIDE):
        for pz in range(SIDE):
            for pc in range(2):
                to = (((px + dx) % SIDE) * SIDE + (pz + dz) % SIDE) * 2 + (pc ^ dc)
                pairs.append(((px * SIDE + pz) * 2 + pc, to))
    return lax.ppermute(x, "vocab", pairs)


def shape(*dims, dtype=F32):
    return jax.ShapeDtypeStruct(dims, dtype)


def cost(flops, moved):
    return pl.CostEstimate(flops=flops, bytes_accessed=moved, transcendentals=0)


def in_vmem(x):
    return pltpu.with_memory_space_constraint(x, pltpu.VMEM)


def in_hbm(x):
    return pltpu.with_memory_space_constraint(x, pltpu.HBM)


def launch(kernel, operands, after=(), *, in_specs, scratch_shapes=(), name, **options):
    used, ignored = len(operands), len(after)

    def body(*refs):
        kernel(*refs[:used], *refs[used + ignored :])

    return pl.pallas_call(
        body,
        in_specs=[*in_specs, *[ANY] * ignored],
        scratch_shapes=list(scratch_shapes),
        compiler_params=PARAMS,
        name=name,
        **options,
    )(*operands, *after)


def encode(x, message, at):
    rows, width = x.shape
    largest = jnp.max(jnp.abs(x), axis=1, keepdims=True)
    power = jnp.clip(jnp.floor(jnp.log2(jnp.maximum(largest, 1e-30))) + 1.0, -100.0, 100.0)
    codes = jnp.clip(jnp.round(x * jnp.exp2(15.0 - power)), -32767.0, 32767.0)
    message[pl.ds(at, rows), :width] = codes.astype(jnp.int32).astype(jnp.int16)
    tail = jnp.broadcast_to(power, (rows, TAIL)).astype(jnp.int32)
    message[pl.ds(at, rows), width:] = tail.astype(jnp.int16)


def decode(message, at, rows):
    width = message.shape[1] - TAIL
    power = message[pl.ds(at, rows), width:].astype(jnp.int32).astype(F32)[:, :1]
    codes = message[pl.ds(at, rows), :width].astype(jnp.int32).astype(F32)
    return codes * jnp.exp2(power - 15.0)


def hold_kernel(head, held, token, sem):
    copy = pltpu.make_async_copy(head, held, sem)
    copy.start()
    token[...] = jnp.zeros_like(token)
    copy.wait()


def hold(head, after=()):
    return launch(
        hold_kernel,
        (head,),
        after,
        out_shape=[pltpu.VMEM(head.shape, head.dtype), shape(8, TAIL)],
        in_specs=[ANY],
        out_specs=[VMEM] * 2,
        scratch_shapes=[pltpu.SemaphoreType.DMA(())],
        cost_estimate=cost(0, 2 * head.size),
        name="hold_head",
    )


def normalise_kernel(place, hidden, gain, targets, *blocks):
    rows, width = hidden.shape
    depth = width // SIDE
    values = hidden[...].astype(F32)
    inverse = lax.rsqrt(jnp.mean(values * values, axis=1, keepdims=True) + EPS)
    lane = lax.broadcasted_iota(jnp.int32, (rows, TAIL), 1)
    row = lax.broadcasted_iota(jnp.int32, (rows, TAIL), 0)
    digits = jnp.zeros((rows, TAIL), jnp.int32)
    for i in range(rows):
        high = targets[i] // 256
        low = targets[i] - high * 256
        digits = jnp.where(row == i, jnp.where(lane == 0, high, jnp.where(lane == 1, low, 0)), digits)
    digits = digits.astype(F32).astype(BF16)
    for step in range(SIDE):
        at = pl.multiple_of(lax.rem(place[0] + step, SIDE) * depth, depth)
        cut = hidden[:, pl.ds(at, depth)].astype(F32) * inverse * gain[:, pl.ds(at, depth)]
        blocks[step][:, :depth] = cut.astype(BF16)
        blocks[step][:, depth:] = digits


def normalise(place, hidden, gain, targets, after=()):
    rows, width = hidden.shape
    return launch(
        normalise_kernel,
        (place, hidden, gain, targets,),
        after,
        out_shape=[shape(rows, width // SIDE + TAIL, dtype=BF16)] * SIDE,
        in_specs=[SMEM, VMEM, VMEM, SMEM],
        out_specs=[VMEM] * SIDE,
        cost_estimate=cost(10 * rows * width, 8 * rows * width),
        name="normalise",
    )


def logits_kernel(offsets, count, *refs):
    pieces, head, refs = refs[:count], refs[count], refs[count + 1 :]
    depth, columns = head.shape
    outs, (rows, sems) = refs[:2], refs[-2:]
    per = rows.shape[1]
    step = pl.program_id(0)

    @pl.when(step == 0)
    def _():
        copies = []
        for i, ds in enumerate(offsets):
            at = 0
            for piece in pieces:
                span = piece.shape[1]
                to = rows.at[i, pl.ds(at, span), :]
                sem = sems.at[len(copies)]
                copies.append(pltpu.make_async_copy(piece.at[ds, :, pl.ds(0, depth)], to, sem))
                at += span
        for copy in copies:
            copy.start()
        for copy in copies:
            copy.wait()

    cut = pl.ds(pl.multiple_of(step * TILE, TILE), TILE)
    part = jnp.dot(rows[...].reshape(-1, depth), head[:, cut], preferred_element_type=F32)
    if offsets != (2,):
        for i in range(len(offsets)):
            outs[i][...] = part[i * per : (i + 1) * per]
        return
    far = refs[2]
    far[:, cut] = part

    @pl.when(step == pl.num_programs(0) - 1)
    def _():
        half = per // 2
        for at in range(0, half, 32):
            encode(far[pl.ds(at, 32), :], outs[0], at)
            encode(far[pl.ds(half + at, 32), :], outs[1], at)


def logits_of(offsets, pieces, head, after=()):
    depth, columns = head.shape
    count, per = len(offsets), sum(p.shape[1] for p in pieces)
    if offsets == (2,):
        outs = [shape(per // 2, columns + TAIL, dtype=jnp.int16)] * 2
        specs = [pl.BlockSpec((per // 2, columns + TAIL), lambda j: (0, 0))] * 2
        scratch = [pltpu.VMEM((per, columns), F32)]
    else:
        outs = [shape(per, columns)] * count
        specs = [pl.BlockSpec((per, TILE), lambda j: (0, j))] * count
        scratch = []
    scratch += [pltpu.VMEM((count, per, depth), BF16), pltpu.SemaphoreType.DMA((count * len(pieces),))]
    kernel = functools.partial(logits_kernel, offsets, len(pieces))
    if count == 1 and offsets != (2,):
        def kernel(*refs):
            at = len(pieces) + 1
            logits_kernel(offsets, len(pieces), *refs[: at + 1], None, *refs[at + 1 :])

    return launch(
        kernel,
        (*pieces, in_vmem(head)),
        after,
        grid=(columns // TILE,),
        out_shape=outs,
        in_specs=[ANY] * len(pieces) + [VMEM],
        out_specs=specs,
        scratch_shapes=scratch,
        cost_estimate=cost(0, 2 * depth * columns + 4 * count * per * columns),
        name="partial_logits",
    )


def pass_on_kernel(first, last, up, down, to_first, to_last):
    per = first.shape[0]
    half = per // 2
    for at in range(0, half, 32):
        encode(first[pl.ds(at, 32), :] + decode(up, at, 32), to_first, at)
        encode(last[pl.ds(at, 32), :], to_last, at)
        encode(first[pl.ds(half + at, 32), :], to_first, half + at)
        encode(last[pl.ds(half + at, 32), :] + decode(down, at, 32), to_last, half + at)


def pass_on(first, last, up, down, after=()):
    per, columns = first.shape
    return launch(
        pass_on_kernel,
        (first, last, up, down,),
        after,
        out_shape=[shape(per, columns + TAIL, dtype=jnp.int16)] * 2,
        in_specs=[VMEM] * 4,
        out_specs=[VMEM] * 2,
        cost_estimate=cost(20 * per * columns, 14 * per * columns),
        name="pass_on",
    )


def onehot_of(place, digits, columns):
    want = digits[:, :1].astype(F32) * 256.0 + digits[:, 1:2].astype(F32)
    want = want.astype(jnp.int32) - place[4]
    return lax.broadcasted_iota(jnp.int32, (digits.shape[0], columns), 1) == want


def own_logits_kernel(count, place, own, below, above, *refs):
    digits, (exps, stats) = refs[: 2 * count], refs[2 * count :]
    per, columns = own.shape
    at = 0
    for digit in digits:
        span = digit.shape[1]
        lane = lax.broadcasted_iota(jnp.int32, (span, TAIL), 1)
        x = own[pl.ds(at, span), :] + (decode(below, at, span) + decode(above, at, span))
        top = jnp.max(x, axis=1, keepdims=True)
        exp = jnp.exp(x - top)
        exps[at // (per // 2), pl.ds(at % (per // 2), span), :] = exp.astype(BF16)
        total = jnp.sum(exp, axis=1, keepdims=True)
        pick = jnp.sum(jnp.where(onehot_of(place, digit[0], columns), x, 0.0), axis=1, keepdims=True)
        stats[pl.ds(at, span), :] = jnp.where(lane == 0, top, jnp.where(lane == 1, total, pick))
        at += span


def digit_specs(pieces):
    at = pieces[0].shape[2] // TAIL - 1
    return [pl.BlockSpec((1, p.shape[1], TAIL), lambda j: (0, 0, at)) for p in pieces]


def own_logits(place, own, below, above, mine, theirs, after=()):
    per, columns = own.shape
    full = pl.BlockSpec((per, columns), lambda j: (0, 0))
    coded = pl.BlockSpec((per, columns + TAIL), lambda j: (0, 0))
    return launch(
        functools.partial(own_logits_kernel, len(mine)),
        (place, own, below, above, *mine, *theirs),
        after,
        grid=(1,),
        out_shape=[shape(2, per // 2, columns, dtype=BF16), shape(per, TAIL)],
        in_specs=[SMEM, full, coded, coded] + digit_specs([*mine, *theirs]),
        out_specs=[pl.BlockSpec((2, per // 2, columns), lambda j: (0, 0, 0)), pl.BlockSpec((per, TAIL), lambda j: (0, 0))],
        cost_estimate=cost(20 * per * columns, 12 * per * columns),
        name="own_logits",
    )


def at_owner(place, dz, dc, dx, size):
    z = lax.rem(place[2] + dz, SIDE)
    x = lax.rem(place[1] + dx, SIDE)
    c = lax.rem(place[3] + dc, 2)
    return pl.multiple_of(((z * 2 + c) * SIDE + x) * size, size)


def walk(groups, size):
    for g, offsets in enumerate(groups):
        at = 0
        for dc in range(2):
            for dz in offsets:
                for dx in range(SIDE):
                    yield g, at, dz, dc, dx
                    at += size


def pack_kernel(groups, size, place, *refs):
    stats, (message, ordered) = refs[: len(groups)], refs[len(groups) :]
    for g, at, dz, dc, dx in walk(groups, size):
        ordered[pl.ds(at_owner(place, dz, dc, dx, size), size), :] = stats[g][pl.ds(at, size), :]
    message[...] = jnp.transpose(ordered[...])[:8]


def pack(place, stats, groups, size, after=()):
    rows = sum(s.shape[0] for s in stats)
    return launch(
        functools.partial(pack_kernel, groups, size),
        (place, *stats,),
        after,
        out_shape=shape(8, rows),
        in_specs=[SMEM] + [VMEM] * len(stats),
        out_specs=VMEM,
        scratch_shapes=[pltpu.VMEM((rows, TAIL), F32)],
        cost_estimate=cost(rows * TAIL, rows * TAIL * 4),
        name="pack_statistics",
    )


def merged(stats):
    tops = [x[:1] for x in stats]
    top = functools.reduce(jnp.maximum, tops)
    totals = [x[1:2] * jnp.exp(t - top) for x, t in zip(stats, tops)]
    picks = [x[2:3] for x in stats]
    if len(stats) == 4:
        totals, picks = ([x[0] + x[2], x[1] + x[3]] for x in (totals, picks))
    return top, totals[0] + totals[1], picks[0] + picks[1]


def merge_kernel(*refs):
    top, total, pick = merged([ref[...] for ref in refs[:-1]])
    row = lax.broadcasted_iota(jnp.int32, refs[-1].shape, 0)
    refs[-1][...] = jnp.where(row == 0, top, jnp.where(row == 1, total, pick))


def merge(stats, after=()):
    return launch(
        merge_kernel,
        (*stats,),
        after,
        out_shape=shape(*stats[0].shape),
        in_specs=[VMEM] * len(stats),
        out_specs=VMEM,
        cost_estimate=cost(64 * stats[0].size, 32 * stats[0].size),
        name="merge_statistics",
    )


def combine_kernel(offsets, size, count, place, weight, *refs):
    parts, (stats, message, ordered, scale) = refs[:count], refs[count:]
    top, total, pick = merged([ref[...] for ref in parts])
    log_total = top + jnp.log(total)
    loss = weight[0] * jnp.sum(log_total - pick, axis=1, keepdims=True)
    ordered[...] = jnp.transpose(jnp.broadcast_to(log_total, (TAIL, log_total.shape[1])))
    for _, at, dz, dc, dx in walk((offsets,), size):
        rows = ordered[pl.ds(at_owner(place, dz, dc, dx, size), size), :]
        scale[pl.ds(at, size), :] = weight[0] * jnp.exp(stats[pl.ds(at, size), :1] - rows)
    scales = jnp.transpose(scale[...])[:8]
    row = lax.broadcasted_iota(jnp.int32, scales.shape, 0)
    message[...] = jnp.where(row == 0, scales, jnp.where(row == 1, weight[0], loss))


def combine(place, weight, parts, stats, offsets, size, after=()):
    rows = stats.shape[0]
    return launch(
        functools.partial(combine_kernel, offsets, size, len(parts)),
        (place, weight, *parts, stats),
        after,
        out_shape=shape(8, rows),
        in_specs=[SMEM, SMEM] + [VMEM] * (len(parts) + 1),
        out_specs=VMEM,
        scratch_shapes=[pltpu.VMEM((rows, TAIL), F32)] * 2,
        cost_estimate=cost(rows * TAIL, rows * TAIL * 4),
        name="combine_statistics",
    )


def halves_kernel(below, above, first, last):
    first[...] = below[0]
    last[...] = above[1]


def halves(below, above, after=()):
    out = shape(*below.shape[1:], dtype=below.dtype)
    return launch(
        halves_kernel,
        (below, above),
        after,
        out_shape=[out] * 2,
        in_specs=[VMEM] * 2,
        out_specs=[VMEM] * 2,
        cost_estimate=cost(0, 4 * below.size),
        name="halves",
    )


def dlogit_kernel(dc, place, *refs):
    scales, (own, above, far, below), digits, out = refs[:SIDE], refs[SIDE : 2 * SIDE], refs[2 * SIDE : -1], refs[-1]
    half, columns = far.shape
    for ds in range(SIDE):
        scale = jnp.transpose(jnp.broadcast_to(scales[ds][:1], (TAIL, 2 * half)))
        weight = scales[ds][1:2, :1]
        at = 0
        for digit in digits:
            span = digit.shape[1]
            exp = far[pl.ds(at, span), :] if ds == 2 else (own, above, None, below)[ds][0, pl.ds(at, span), :]
            hit = onehot_of(place, digit[ds], columns)
            factor = scale[dc * half + at : dc * half + at + span, :1]
            grad = exp.astype(F32) * factor - jnp.where(hit, weight, 0.0)
            out[ds, pl.ds(at, span), :] = grad.astype(BF16)
            at += span


def dlogit_of(dc, place, scales, own, above, far, below, pieces, after=()):
    half, columns = far.shape
    at = pieces[0].shape[2] // TAIL - 1
    one = pl.BlockSpec((1, half, columns), lambda j: (dc, 0, 0))
    return launch(
        functools.partial(dlogit_kernel, dc),
        (place, *scales, own, above, far, below, *pieces),
        after,
        grid=(1,),
        out_shape=shape(SIDE, half, columns, dtype=BF16),
        in_specs=[SMEM]
        + [pl.BlockSpec(scales[0].shape, lambda j: (0, 0))] * SIDE
        + [one, one, pl.BlockSpec((half, columns), lambda j: (0, 0)), one]
        + [pl.BlockSpec((SIDE, p.shape[1], TAIL), lambda j: (0, 0, at)) for p in pieces],
        out_specs=pl.BlockSpec((SIDE, half, columns), lambda j: (0, 0, 0)),
        cost_estimate=cost(40 * half * columns, 16 * half * columns),
        name="dlogit",
    )


def dnormed_kernel(first, count, left, right, head, other, *refs):
    normed, outs, gain = refs[: -1 - count], refs[-1 - count : -1], refs[-1]
    columns = head.shape[1]
    dims = (((1,), (1,)), ((), ()))
    cut = pl.ds(pl.multiple_of(pl.program_id(0) * TILE, TILE), TILE)
    span = outs[0].shape[1]
    rows = pl.ds(first, count * span)
    part = lax.dot_general(left[:, rows, :].reshape(-1, columns), head[cut, :], dims, preferred_element_type=F32)
    part = part + lax.dot_general(
        right[:, rows, :].reshape(-1, columns), other[cut, :], dims, preferred_element_type=F32
    )
    x = jnp.concatenate([n[...] for n in normed], axis=1).reshape(part.shape).astype(F32)
    gain[...] = jnp.sum((part * x).reshape(-1, 8, TILE), axis=0)
    part = part.reshape(SIDE, count, -1, TILE)
    for k in range(count):
        outs[k][...] = part[:, k].astype(outs[k].dtype)


def dnormed_of(first, left, right, head, other, normed, span, dtype, after=()):
    depth, columns = head.shape
    count = sum(n.shape[1] for n in normed) // span
    block = pl.BlockSpec((SIDE, span, TILE), lambda j: (0, 0, j))
    return launch(
        functools.partial(dnormed_kernel, first, count),
        (left, right, in_vmem(head), in_vmem(other), *normed),
        after,
        grid=(depth // TILE,),
        out_shape=[shape(SIDE, span, depth, dtype=dtype)] * count + [shape(8, depth)],
        in_specs=[VMEM] * 4 + [pl.BlockSpec((SIDE, n.shape[1], TILE), lambda j: (0, 0, j)) for n in normed],
        out_specs=[block] * count + [pl.BlockSpec((8, TILE), lambda j: (0, j))],
        cost_estimate=cost(0, 4 * depth * columns),
        name="dnormed",
    )


def head_grad_kernel(count, *refs):
    pieces, (ours, others) = refs[:count], refs[count : count + 2]
    out, token, grads, sems = refs[-4:]
    token[...] = jnp.zeros_like(token)

    @pl.when(pl.program_id(0) == 0)
    def _():
        copies = [(ours, grads.at[:, 0]), (others, grads.at[:, 1])]
        copies = [pltpu.make_async_copy(a, b, sems.at[i]) for i, (a, b) in enumerate(copies)]
        for copy in copies:
            copy.start()
        for copy in copies:
            copy.wait()

    x = jnp.concatenate([piece[...] for piece in pieces], axis=1).reshape(-1, TILE)
    y = grads[...].reshape(x.shape[0], -1)
    out[...] = lax.dot_general(x, y, (((0,), (0,)), ((), ())), preferred_element_type=F32).astype(BF16)


def head_grad_of(pieces, ours, others, depth, start, stop, into=None, after=()):
    columns, rows = ours.shape[2], 2 * SIDE * ours.shape[1]
    inputs = [in_hbm(x) for x in (*pieces, ours, others)]
    specs = [pl.BlockSpec((SIDE, p.shape[1], TILE), lambda j: (0, 0, start + j)) for p in pieces] + [ANY] * 2
    aliases = {}
    if into is not None:
        aliases = {len(inputs): 0}
        inputs.append(in_hbm(into))
        specs.append(ANY)
    return launch(
        functools.partial(head_grad_kernel, len(pieces)),
        (*inputs,),
        after,
        grid=(stop - start,),
        input_output_aliases=aliases,
        out_shape=[shape(depth, columns, dtype=BF16), shape(8, TAIL)],
        in_specs=specs,
        out_specs=[pl.BlockSpec((TILE, columns), lambda j: (start + j, 0)), pl.BlockSpec((8, TAIL), lambda j: (0, 0))],
        scratch_shapes=[pltpu.VMEM((SIDE, 2, *ours.shape[1:]), BF16), pltpu.SemaphoreType.DMA((2,))],
        cost_estimate=cost(2 * rows * (stop - start) * TILE * columns, depth * columns + 4 * rows * depth),
        name="head_grad",
    )


def spread_kernel(near, own, out):
    gain = jnp.sum(near[...] + own[...], axis=0, keepdims=True)
    wide = out.shape[2]
    gain = jnp.concatenate([gain[:, i * wide : (i + 1) * wide] for i in range(out.shape[1])], axis=0)
    out[...] = jnp.broadcast_to(gain, out.shape)


def spread(near, own, after=()):
    rows, depth = near.shape
    return launch(
        spread_kernel,
        (near, own),
        after,
        out_shape=shape(8 * SIDE, rows, depth // rows),
        in_specs=[VMEM] * 2,
        out_specs=VMEM,
        cost_estimate=cost(rows * depth, 4 * 8 * SIDE * depth),
        name="gain_parts",
    )


def to_x_kernel(own, far, up, down, block, *messages):
    total = (own[...] + far[...].astype(F32)) + (up[...].astype(F32) + down[...].astype(F32))
    rows = own.shape[1] // SIDE
    for dx in range(SIDE):
        cut = jnp.concatenate([total[ds, dx * rows : (dx + 1) * rows] for ds in range(SIDE)], axis=0)
        if dx == 0:
            block[...] = cut
        else:
            messages[dx - 1][...] = cut.astype(BF16)


def to_x(own, far, up, down, after=()):
    _, span, depth = own.shape
    return launch(
        to_x_kernel,
        (own, far, up, down),
        after,
        out_shape=[shape(span, depth)] + [shape(span, depth, dtype=BF16)] * 3,
        in_specs=[VMEM] * 4,
        out_specs=[VMEM] * 4,
        cost_estimate=cost(8 * span * depth, 48 * span * depth),
        name="over_x",
    )


def to_y_kernel(place, block, up, far, down, gains, loss, message):
    span, depth = block.shape
    total = (block[...] + far[...].astype(F32)) + (up[...].astype(F32) + down[...].astype(F32))
    gain = jnp.sum(gains[...], axis=0)
    gain = jnp.concatenate([gain[i : i + 1] for i in range(gain.shape[0])], axis=1)
    rows = span // SIDE
    row = lax.broadcasted_iota(jnp.int32, (rows, depth), 0)
    extra = jnp.where(row == 0, gain, jnp.where(row == 1, loss[2:3, :1], 0.0))
    for ds in range(SIDE):
        filled = jnp.concatenate([total[ds * rows : (ds + 1) * rows], extra], axis=0)
        message[lax.rem(place[0] + ds, SIDE)] = filled


def to_y(place, block, up, far, down, gains, loss, after=()):
    span, depth = block.shape
    return launch(
        to_y_kernel,
        (place, block, up, far, down, gains, loss),
        after,
        out_shape=shape(SIDE, 2 * span // SIDE, depth),
        in_specs=[SMEM] + [VMEM] * 6,
        out_specs=VMEM,
        cost_estimate=cost(8 * span * depth, 16 * span * depth),
        name="over_y",
    )


def finish_kernel(hidden, gain, message, out, gain_out, loss_out, dnormed):
    rows, width = hidden.shape
    depth = width // SIDE
    for s in range(SIDE):
        cut = pl.ds(s * depth, depth)
        dnormed[:, cut] = message[s, :rows]
        gain_out[:, cut] = message[s, rows : rows + 1] / gain[:, cut]
    loss = message[:, rows + 1, :TAIL]
    loss_out[...] = jnp.sum(loss, axis=0, keepdims=True)
    values = hidden[...].astype(F32)
    inverse = lax.rsqrt(jnp.mean(values * values, axis=1, keepdims=True) + EPS)
    gained = dnormed[...] * gain[...]
    inner = jnp.mean(gained * values, axis=1, keepdims=True)
    out[...] = (inverse * gained - values * (inverse * inverse * inverse) * inner).astype(BF16)


def finish(hidden, gain, message, after=()):
    rows, width = hidden.shape
    return launch(
        finish_kernel,
        (hidden, gain, message),
        after,
        out_shape=[shape(rows, width, dtype=BF16), shape(1, width), shape(1, TAIL)],
        in_specs=[VMEM] * 3,
        out_specs=[VMEM] * 3,
        scratch_shapes=[pltpu.VMEM((rows, width), F32)],
        cost_estimate=cost(12 * rows * width, 16 * rows * width),
        name="finish",
    )


def section_weights(exit_layer, numerators):
    layers = numerators.shape[0]
    matches = exit_layer[:, None] == jnp.arange(layers, dtype=jnp.int32)[None, :]
    picked = jnp.sum(jnp.where(matches, numerators[None, :], 0), axis=1).astype(F32)
    return picked / jnp.sum(picked)


def local(hidden_rows, norm_gain, head_weight, targets, exit_layer, numerators):
    section, piece = lax.axis_index("section"), lax.axis_index("vocab")
    own_rows, width = hidden_rows.shape
    depth, columns = head_weight.shape
    place = jnp.stack([section, piece // 8, (piece // 2) % SIDE, piece % 2, piece * columns]).astype(jnp.int32)
    gain_row = norm_gain.reshape(1, width)
    weights = section_weights(exit_layer, numerators)
    weight = jnp.sum(jnp.where(jnp.arange(SIDE) == section, weights, 0.0)).reshape(1)

    cuts = normalise(place, in_hbm(hidden_rows), in_hbm(gain_row), targets)
    own = jnp.stack([cuts[0], over_section(cuts[3], -1), over_section(cuts[2], 2), over_section(cuts[1], 1)])
    def along_x(x):
        return [x, over_vocab(x, dx=-1), over_vocab(x, dx=2), over_vocab(x, dx=1)]

    pair = jnp.stack([over_vocab(own, dz=-1), over_vocab(own, dz=1)], axis=1)
    mine = [jnp.concatenate(along_x(own), axis=1)]
    held_head, token = hold(head_weight, (own,))
    *pair, _ = lax.optimization_barrier((*along_x(pair), token))
    mine.append(jnp.stack(pair, axis=2).reshape(SIDE, -1, own.shape[2]))
    mine.append(over_vocab(mine[0], dz=2))
    theirs = [over_vocab(m, dc=1) for m in mine]
    pieces = (*mine, *theirs)
    groups = ((0,), (1, 3), (2,))
    everything = (sum(groups, ()),)

    up, down = logits_of((2,), pieces, held_head)
    head_ready, _ = lax.optimization_barrier((head_weight, up))
    other_head = over_vocab(head_ready, dc=1)
    first, last = logits_of((1, 3), pieces, held_head, (up,))
    up, down = over_section(up, 1), over_section(down, -1)
    first, last = pass_on(first, last, up, down)
    (kept,) = logits_of((0,), pieces, held_head, (first,))
    below, above = over_section(first, 1), over_section(last, -1)
    exps, stats = own_logits(place, kept, below, above, mine, theirs)

    below, above = over_section(exps, 1), over_section(exps, -1)
    held_other, token = hold(other_head, (stats,))
    parts = pack(place, [stats], everything, own_rows, (token,))
    parts = merge([parts, over_vocab(parts, dc=1)])
    parts = merge(along_x(parts))
    far_first, far_last = halves(below, above, (parts, token))
    far_first, far_last = over_section(far_first, 1), over_section(far_last, -1)
    parts = [parts, over_vocab(parts, dz=-1), over_vocab(parts, dz=2), over_vocab(parts, dz=1)]
    scales = combine(place, weight, parts, stats, everything[0], own_rows)
    loss = scales
    scales = [scales, over_section(scales, -1), over_section(scales, 2), over_section(scales, 1)]

    others = dlogit_of(1, place, scales, exps, above, far_last, below, theirs, (far_first,))
    swapped = over_vocab(others, dc=1)
    ours = dlogit_of(0, place, scales, exps, above, far_first, below, mine, (others,))
    span = mine[0].shape[1]
    to_up, to_down, to_far, gain_near = dnormed_of(
        span, ours, swapped, held_head, held_other, mine[1:], span, BF16
    )
    moved = [over_vocab(to_far, dz=2), over_vocab(to_up, dz=1), over_vocab(to_down, dz=-1)]
    kept, gain_own = dnormed_of(0, ours, swapped, held_head, held_other, mine[:1], span, F32, (gain_near,))

    gains = lax.all_to_all(spread(gain_near, gain_own), "vocab", 0, 0)
    tiles = depth // TILE
    grad, token = head_grad_of(pieces, ours, others, depth, 0, tiles // 2, None, (gain_own,))
    block, *cuts = to_x(kept, *moved, (token,))
    cuts = [over_vocab(cuts[0], dx=1), over_vocab(cuts[1], dx=2), over_vocab(cuts[2], dx=-1)]
    grad, token = head_grad_of(pieces, ours, others, depth, tiles // 2, 3 * tiles // 4, grad, (block,))
    message = to_y(place, block, *cuts, gains, loss, (token,))
    got = lax.all_to_all(message, "section", 0, 0)
    head_grad, token = head_grad_of(pieces, ours, others, depth, 3 * tiles // 4, tiles, grad, (message,))
    hidden_grad, gain_grad, total_loss = finish(hidden_rows, gain_row, got, (token,))
    return (hidden_grad, gain_grad.reshape(width), head_grad, total_loss[0, 0])


def solution(mesh):
    return jax.shard_map(
        local,
        mesh=mesh,
        in_specs=(
            P(("section", "vocab"), None),
            P(),
            P("section", "vocab"),
            P(("section", "vocab")),
            P(),
            P(),
        ),
        out_specs=(P(("section", "vocab"), None), P(), P("section", "vocab"), P()),
        check_vma=False,
    )
```

```python
import functools
import jax
import jax.numpy as jnp
from jax import lax
from jax.experimental import pallas as pl
from jax.experimental.pallas import tpu as pltpu
from jax.sharding import PartitionSpec as P

EPS = 1e-05
SIDE = 4
TAIL = 128
TILE = 256
F32 = jnp.float32
BF16 = jnp.bfloat16
ANY = pl.BlockSpec(memory_space=pl.ANY)
VMEM = pl.BlockSpec(memory_space=pltpu.VMEM)
SMEM = pl.BlockSpec(memory_space=pltpu.SMEM)
PARAMS = pltpu.CompilerParams(vmem_limit_bytes=22 * 2**20)


def over_section(x, step):
    return lax.ppermute(x, "section", [(i, (i + step) % SIDE) for i in range(SIDE)])


def over_vocab(x, dx=0, dz=0, dc=0):
    pairs = []
    for px in range(SIDE):
        for pz in range(SIDE):
            for pc in range(2):
                to = (((px + dx) % SIDE) * SIDE + (pz + dz) % SIDE) * 2 + (pc ^ dc)
                pairs.append(((px * SIDE + pz) * 2 + pc, to))
    return lax.ppermute(x, "vocab", pairs)


def shape(*dims, dtype=F32):
    return jax.ShapeDtypeStruct(dims, dtype)


def cost(flops, moved):
    return pl.CostEstimate(flops=flops, bytes_accessed=moved, transcendentals=0)


def in_vmem(x):
    return pltpu.with_memory_space_constraint(x, pltpu.VMEM)


def in_hbm(x):
    return pltpu.with_memory_space_constraint(x, pltpu.HBM)


def launch(kernel, operands, after=(), *, in_specs, scratch_shapes=(), name, **options):
    used, ignored = len(operands), len(after)

    def body(*refs):
        kernel(*refs[:used], *refs[used + ignored :])

    return pl.pallas_call(
        body,
        in_specs=[*in_specs, *[ANY] * ignored],
        scratch_shapes=list(scratch_shapes),
        compiler_params=PARAMS,
        name=name,
        **options,
    )(*operands, *after)


def encode(x, message, at):
    rows, width = x.shape
    largest = jnp.max(jnp.abs(x), axis=1, keepdims=True)
    power = jnp.clip(jnp.floor(jnp.log2(jnp.maximum(largest, 1e-30))) + 1.0, -100.0, 100.0)
    codes = jnp.clip(jnp.round(x * jnp.exp2(15.0 - power)), -32767.0, 32767.0)
    message[pl.ds(at, rows), :width] = codes.astype(jnp.int32).astype(jnp.int16)
    tail = jnp.broadcast_to(power, (rows, TAIL)).astype(jnp.int32)
    message[pl.ds(at, rows), width:] = tail.astype(jnp.int16)


def decode(message, at, rows):
    width = message.shape[1] - TAIL
    power = message[pl.ds(at, rows), width:].astype(jnp.int32).astype(F32)[:, :1]
    codes = message[pl.ds(at, rows), :width].astype(jnp.int32).astype(F32)
    return codes * jnp.exp2(power - 15.0)


def hold_kernel(head, held, token, sem):
    copy = pltpu.make_async_copy(head, held, sem)
    copy.start()
    token[...] = jnp.zeros_like(token)
    copy.wait()


def hold(head, after=()):
    return launch(
        hold_kernel,
        (head,),
        after,
        out_shape=[pltpu.VMEM(head.shape, head.dtype), shape(8, TAIL)],
        in_specs=[ANY],
        out_specs=[VMEM] * 2,
        scratch_shapes=[pltpu.SemaphoreType.DMA(())],
        cost_estimate=cost(0, 2 * head.size),
        name="hold_head",
    )


def normalise_kernel(place, hidden, gain, targets, *blocks):
    rows, width = hidden.shape
    depth = width // SIDE
    values = hidden[...].astype(F32)
    inverse = lax.rsqrt(jnp.mean(values * values, axis=1, keepdims=True) + EPS)
    lane = lax.broadcasted_iota(jnp.int32, (rows, TAIL), 1)
    row = lax.broadcasted_iota(jnp.int32, (rows, TAIL), 0)
    digits = jnp.zeros((rows, TAIL), jnp.int32)
    for i in range(rows):
        high = targets[i] // 256
        low = targets[i] - high * 256
        digits = jnp.where(row == i, jnp.where(lane == 0, high, jnp.where(lane == 1, low, 0)), digits)
    digits = digits.astype(F32).astype(BF16)
    for step in range(SIDE):
        at = pl.multiple_of(lax.rem(place[0] + step, SIDE) * depth, depth)
        cut = hidden[:, pl.ds(at, depth)].astype(F32) * inverse * gain[:, pl.ds(at, depth)]
        blocks[step][:, :depth] = cut.astype(BF16)
        blocks[step][:, depth:] = digits


def normalise(place, hidden, gain, targets, after=()):
    rows, width = hidden.shape
    return launch(
        normalise_kernel,
        (place, hidden, gain, targets,),
        after,
        out_shape=[shape(rows, width // SIDE + TAIL, dtype=BF16)] * SIDE,
        in_specs=[SMEM, VMEM, VMEM, SMEM],
        out_specs=[VMEM] * SIDE,
        cost_estimate=cost(10 * rows * width, 8 * rows * width),
        name="normalise",
    )


def logits_kernel(offsets, count, *refs):
    pieces, head, refs = refs[:count], refs[count], refs[count + 1 :]
    depth, columns = head.shape
    outs, (rows, sems) = refs[:2], refs[-2:]
    per = rows.shape[1]
    step = pl.program_id(0)

    @pl.when(step == 0)
    def _():
        copies = []
        for i, ds in enumerate(offsets):
            at = 0
            for piece in pieces:
                span = piece.shape[1]
                to = rows.at[i, pl.ds(at, span), :]
                sem = sems.at[len(copies)]
                copies.append(pltpu.make_async_copy(piece.at[ds, :, pl.ds(0, depth)], to, sem))
                at += span
        for copy in copies:
            copy.start()
        for copy in copies:
            copy.wait()

    cut = pl.ds(pl.multiple_of(step * TILE, TILE), TILE)
    part = jnp.dot(rows[...].reshape(-1, depth), head[:, cut], preferred_element_type=F32)
    if offsets != (2,):
        for i in range(len(offsets)):
            outs[i][...] = part[i * per : (i + 1) * per]
        return
    far = refs[2]
    far[:, cut] = part

    @pl.when(step == pl.num_programs(0) - 1)
    def _():
        half = per // 2
        for at in range(0, half, 32):
            encode(far[pl.ds(at, 32), :], outs[0], at)
            encode(far[pl.ds(half + at, 32), :], outs[1], at)


def logits_of(offsets, pieces, head, after=()):
    depth, columns = head.shape
    count, per = len(offsets), sum(p.shape[1] for p in pieces)
    if offsets == (2,):
        outs = [shape(per // 2, columns + TAIL, dtype=jnp.int16)] * 2
        specs = [pl.BlockSpec((per // 2, columns + TAIL), lambda j: (0, 0))] * 2
        scratch = [pltpu.VMEM((per, columns), F32)]
    else:
        outs = [shape(per, columns)] * count
        specs = [pl.BlockSpec((per, TILE), lambda j: (0, j))] * count
        scratch = []
    scratch += [pltpu.VMEM((count, per, depth), BF16), pltpu.SemaphoreType.DMA((count * len(pieces),))]
    kernel = functools.partial(logits_kernel, offsets, len(pieces))
    if count == 1 and offsets != (2,):
        def kernel(*refs):
            at = len(pieces) + 1
            logits_kernel(offsets, len(pieces), *refs[: at + 1], None, *refs[at + 1 :])

    return launch(
        kernel,
        (*pieces, in_vmem(head)),
        after,
        grid=(columns // TILE,),
        out_shape=outs,
        in_specs=[ANY] * len(pieces) + [VMEM],
        out_specs=specs,
        scratch_shapes=scratch,
        cost_estimate=cost(0, 2 * depth * columns + 4 * count * per * columns),
        name="partial_logits",
    )


def pass_on_kernel(first, last, up, down, to_first, to_last):
    per = first.shape[0]
    half = per // 2
    for at in range(0, half, 32):
        encode(first[pl.ds(at, 32), :] + decode(up, at, 32), to_first, at)
        encode(last[pl.ds(at, 32), :], to_last, at)
        encode(first[pl.ds(half + at, 32), :], to_first, half + at)
        encode(last[pl.ds(half + at, 32), :] + decode(down, at, 32), to_last, half + at)


def pass_on(first, last, up, down, after=()):
    per, columns = first.shape
    return launch(
        pass_on_kernel,
        (first, last, up, down,),
        after,
        out_shape=[shape(per, columns + TAIL, dtype=jnp.int16)] * 2,
        in_specs=[VMEM] * 4,
        out_specs=[VMEM] * 2,
        cost_estimate=cost(20 * per * columns, 14 * per * columns),
        name="pass_on",
    )


def onehot_of(place, digits, columns):
    want = digits[:, :1].astype(F32) * 256.0 + digits[:, 1:2].astype(F32)
    want = want.astype(jnp.int32) - place[4]
    return lax.broadcasted_iota(jnp.int32, (digits.shape[0], columns), 1) == want


def own_logits_kernel(count, place, own, below, above, *refs):
    digits, (exps, stats) = refs[: 2 * count], refs[2 * count :]
    per, columns = own.shape
    at = 0
    for digit in digits:
        span = digit.shape[1]
        lane = lax.broadcasted_iota(jnp.int32, (span, TAIL), 1)
        x = own[pl.ds(at, span), :] + (decode(below, at, span) + decode(above, at, span))
        top = jnp.max(x, axis=1, keepdims=True)
        exp = jnp.exp(x - top)
        exps[at // (per // 2), pl.ds(at % (per // 2), span), :] = exp.astype(BF16)
        total = jnp.sum(exp, axis=1, keepdims=True)
        pick = jnp.sum(jnp.where(onehot_of(place, digit[0], columns), x, 0.0), axis=1, keepdims=True)
        stats[pl.ds(at, span), :] = jnp.where(lane == 0, top, jnp.where(lane == 1, total, pick))
        at += span


def digit_specs(pieces):
    at = pieces[0].shape[2] // TAIL - 1
    return [pl.BlockSpec((1, p.shape[1], TAIL), lambda j: (0, 0, at)) for p in pieces]


def own_logits(place, own, below, above, mine, theirs, after=()):
    per, columns = own.shape
    full = pl.BlockSpec((per, columns), lambda j: (0, 0))
    coded = pl.BlockSpec((per, columns + TAIL), lambda j: (0, 0))
    return launch(
        functools.partial(own_logits_kernel, len(mine)),
        (place, own, below, above, *mine, *theirs),
        after,
        grid=(1,),
        out_shape=[shape(2, per // 2, columns, dtype=BF16), shape(per, TAIL)],
        in_specs=[SMEM, full, coded, coded] + digit_specs([*mine, *theirs]),
        out_specs=[pl.BlockSpec((2, per // 2, columns), lambda j: (0, 0, 0)), pl.BlockSpec((per, TAIL), lambda j: (0, 0))],
        cost_estimate=cost(20 * per * columns, 12 * per * columns),
        name="own_logits",
    )


def at_owner(place, dz, dc, dx, size):
    z = lax.rem(place[2] + dz, SIDE)
    x = lax.rem(place[1] + dx, SIDE)
    c = lax.rem(place[3] + dc, 2)
    return pl.multiple_of(((z * 2 + c) * SIDE + x) * size, size)


def walk(groups, size):
    for g, offsets in enumerate(groups):
        at = 0
        for dc in range(2):
            for dz in offsets:
                for dx in range(SIDE):
                    yield g, at, dz, dc, dx
                    at += size


def pack_kernel(groups, size, place, *refs):
    stats, (message, ordered) = refs[: len(groups)], refs[len(groups) :]
    for g, at, dz, dc, dx in walk(groups, size):
        ordered[pl.ds(at_owner(place, dz, dc, dx, size), size), :] = stats[g][pl.ds(at, size), :]
    message[...] = jnp.transpose(ordered[...])[:8]


def pack(place, stats, groups, size, after=()):
    rows = sum(s.shape[0] for s in stats)
    return launch(
        functools.partial(pack_kernel, groups, size),
        (place, *stats,),
        after,
        out_shape=shape(8, rows),
        in_specs=[SMEM] + [VMEM] * len(stats),
        out_specs=VMEM,
        scratch_shapes=[pltpu.VMEM((rows, TAIL), F32)],
        cost_estimate=cost(rows * TAIL, rows * TAIL * 4),
        name="pack_statistics",
    )


def merged(stats):
    tops = [x[:1] for x in stats]
    top = functools.reduce(jnp.maximum, tops)
    totals = [x[1:2] * jnp.exp(t - top) for x, t in zip(stats, tops)]
    picks = [x[2:3] for x in stats]
    if len(stats) == 4:
        totals, picks = ([x[0] + x[2], x[1] + x[3]] for x in (totals, picks))
    return top, totals[0] + totals[1], picks[0] + picks[1]


def merge_kernel(*refs):
    top, total, pick = merged([ref[...] for ref in refs[:-1]])
    row = lax.broadcasted_iota(jnp.int32, refs[-1].shape, 0)
    refs[-1][...] = jnp.where(row == 0, top, jnp.where(row == 1, total, pick))


def merge(stats, after=()):
    return launch(
        merge_kernel,
        (*stats,),
        after,
        out_shape=shape(*stats[0].shape),
        in_specs=[VMEM] * len(stats),
        out_specs=VMEM,
        cost_estimate=cost(64 * stats[0].size, 32 * stats[0].size),
        name="merge_statistics",
    )


def combine_kernel(offsets, size, count, place, weight, *refs):
    parts, (stats, message, ordered, scale) = refs[:count], refs[count:]
    top, total, pick = merged([ref[...] for ref in parts])
    log_total = top + jnp.log(total)
    loss = weight[0] * jnp.sum(log_total - pick, axis=1, keepdims=True)
    ordered[...] = jnp.transpose(jnp.broadcast_to(log_total, (TAIL, log_total.shape[1])))
    for _, at, dz, dc, dx in walk((offsets,), size):
        rows = ordered[pl.ds(at_owner(place, dz, dc, dx, size), size), :]
        scale[pl.ds(at, size), :] = weight[0] * jnp.exp(stats[pl.ds(at, size), :1] - rows)
    scales = jnp.transpose(scale[...])[:8]
    row = lax.broadcasted_iota(jnp.int32, scales.shape, 0)
    message[...] = jnp.where(row == 0, scales, jnp.where(row == 1, weight[0], loss))


def combine(place, weight, parts, stats, offsets, size, after=()):
    rows = stats.shape[0]
    return launch(
        functools.partial(combine_kernel, offsets, size, len(parts)),
        (place, weight, *parts, stats),
        after,
        out_shape=shape(8, rows),
        in_specs=[SMEM, SMEM] + [VMEM] * (len(parts) + 1),
        out_specs=VMEM,
        scratch_shapes=[pltpu.VMEM((rows, TAIL), F32)] * 2,
        cost_estimate=cost(rows * TAIL, rows * TAIL * 4),
        name="combine_statistics",
    )


def halves_kernel(below, above, first, last):
    first[...] = below[0]
    last[...] = above[1]


def halves(below, above, after=()):
    out = shape(*below.shape[1:], dtype=below.dtype)
    return launch(
        halves_kernel,
        (below, above),
        after,
        out_shape=[out] * 2,
        in_specs=[VMEM] * 2,
        out_specs=[VMEM] * 2,
        cost_estimate=cost(0, 4 * below.size),
        name="halves",
    )


def dlogit_kernel(dc, place, *refs):
    scales, (own, above, far, below), digits, out = refs[:SIDE], refs[SIDE : 2 * SIDE], refs[2 * SIDE : -1], refs[-1]
    half, columns = far.shape
    for ds in range(SIDE):
        scale = jnp.transpose(jnp.broadcast_to(scales[ds][:1], (TAIL, 2 * half)))
        weight = scales[ds][1:2, :1]
        at = 0
        for digit in digits:
            span = digit.shape[1]
            exp = far[pl.ds(at, span), :] if ds == 2 else (own, above, None, below)[ds][0, pl.ds(at, span), :]
            hit = onehot_of(place, digit[ds], columns)
            factor = scale[dc * half + at : dc * half + at + span, :1]
            grad = exp.astype(F32) * factor - jnp.where(hit, weight, 0.0)
            out[ds, pl.ds(at, span), :] = grad.astype(BF16)
            at += span


def dlogit_of(dc, place, scales, own, above, far, below, pieces, after=()):
    half, columns = far.shape
    at = pieces[0].shape[2] // TAIL - 1
    one = pl.BlockSpec((1, half, columns), lambda j: (dc, 0, 0))
    return launch(
        functools.partial(dlogit_kernel, dc),
        (place, *scales, own, above, far, below, *pieces),
        after,
        grid=(1,),
        out_shape=shape(SIDE, half, columns, dtype=BF16),
        in_specs=[SMEM]
        + [pl.BlockSpec(scales[0].shape, lambda j: (0, 0))] * SIDE
        + [one, one, pl.BlockSpec((half, columns), lambda j: (0, 0)), one]
        + [pl.BlockSpec((SIDE, p.shape[1], TAIL), lambda j: (0, 0, at)) for p in pieces],
        out_specs=pl.BlockSpec((SIDE, half, columns), lambda j: (0, 0, 0)),
        cost_estimate=cost(40 * half * columns, 16 * half * columns),
        name="dlogit",
    )


def dnormed_kernel(count, left, right, head, other, *refs):
    normed, outs, gain = refs[: -1 - count], refs[-1 - count : -1], refs[-1]
    columns = head.shape[1]
    dims = (((1,), (1,)), ((), ()))
    cut = pl.ds(pl.multiple_of(pl.program_id(0) * TILE, TILE), TILE)
    part = lax.dot_general(left[...].reshape(-1, columns), head[cut, :], dims, preferred_element_type=F32)
    part = part + lax.dot_general(
        right[...].reshape(-1, columns), other[cut, :], dims, preferred_element_type=F32
    )
    x = jnp.concatenate([n[...] for n in normed], axis=1).reshape(part.shape).astype(F32)
    gain[...] = jnp.sum((part * x).reshape(-1, 8, TILE), axis=0)
    part = part.reshape(SIDE, count, -1, TILE)
    for k in range(count):
        outs[k][...] = part[:, k].astype(outs[k].dtype)


def dnormed_of(left, right, head, other, normed, span, after=()):
    depth, columns = head.shape
    count = sum(n.shape[1] for n in normed) // span
    block = pl.BlockSpec((SIDE, span, TILE), lambda j: (0, 0, j))
    return launch(
        functools.partial(dnormed_kernel, count),
        (left, right, in_vmem(head), in_vmem(other), *normed),
        after,
        grid=(depth // TILE,),
        out_shape=[shape(SIDE, span, depth, dtype=BF16 if k else F32) for k in range(count)] + [shape(8, depth)],
        in_specs=[VMEM] * 4 + [pl.BlockSpec((SIDE, n.shape[1], TILE), lambda j: (0, 0, j)) for n in normed],
        out_specs=[block] * count + [pl.BlockSpec((8, TILE), lambda j: (0, j))],
        cost_estimate=cost(0, 4 * depth * columns),
        name="dnormed",
    )


def head_grad_kernel(count, *refs):
    pieces, (ours, others) = refs[:count], refs[count : count + 2]
    out, token, grads, sems = refs[-4:]
    token[...] = jnp.zeros_like(token)

    @pl.when(pl.program_id(0) == 0)
    def _():
        copies = [(ours, grads.at[:, 0]), (others, grads.at[:, 1])]
        copies = [pltpu.make_async_copy(a, b, sems.at[i]) for i, (a, b) in enumerate(copies)]
        for copy in copies:
            copy.start()
        for copy in copies:
            copy.wait()

    x = jnp.concatenate([piece[...] for piece in pieces], axis=1).reshape(-1, TILE)
    y = grads[...].reshape(x.shape[0], -1)
    out[...] = lax.dot_general(x, y, (((0,), (0,)), ((), ())), preferred_element_type=F32).astype(BF16)


def head_grad_of(pieces, ours, others, depth, after=()):
    columns, rows = ours.shape[2], 2 * SIDE * ours.shape[1]
    return launch(
        functools.partial(head_grad_kernel, len(pieces)),
        tuple(in_hbm(x) for x in (*pieces, ours, others)),
        after,
        grid=(depth // TILE,),
        out_shape=[shape(depth, columns, dtype=BF16), shape(8, TAIL)],
        in_specs=[pl.BlockSpec((SIDE, p.shape[1], TILE), lambda j: (0, 0, j)) for p in pieces] + [ANY] * 2,
        out_specs=[pl.BlockSpec((TILE, columns), lambda j: (j, 0)), pl.BlockSpec((8, TAIL), lambda j: (0, 0))],
        scratch_shapes=[pltpu.VMEM((SIDE, 2, *ours.shape[1:]), BF16), pltpu.SemaphoreType.DMA((2,))],
        cost_estimate=cost(2 * rows * depth * columns, 2 * depth * columns + 4 * rows * depth),
        name="head_grad",
    )


def spread_kernel(terms, out):
    gain = jnp.sum(terms[...], axis=0, keepdims=True)
    wide = out.shape[2]
    gain = jnp.concatenate([gain[:, i * wide : (i + 1) * wide] for i in range(out.shape[1])], axis=0)
    out[...] = jnp.broadcast_to(gain, out.shape)


def spread(terms, after=()):
    rows, depth = terms.shape
    return launch(
        spread_kernel,
        (terms,),
        after,
        out_shape=shape(8 * SIDE, rows, depth // rows),
        in_specs=[VMEM],
        out_specs=VMEM,
        cost_estimate=cost(rows * depth, 4 * 8 * SIDE * depth),
        name="gain_parts",
    )


def to_x_kernel(own, far, up, down, block, *messages):
    total = (own[...] + far[...].astype(F32)) + (up[...].astype(F32) + down[...].astype(F32))
    rows = own.shape[1] // SIDE
    for dx in range(SIDE):
        cut = jnp.concatenate([total[ds, dx * rows : (dx + 1) * rows] for ds in range(SIDE)], axis=0)
        if dx == 0:
            block[...] = cut
        else:
            messages[dx - 1][...] = cut.astype(BF16)


def to_x(own, far, up, down, after=()):
    _, span, depth = own.shape
    return launch(
        to_x_kernel,
        (own, far, up, down),
        after,
        out_shape=[shape(span, depth)] + [shape(span, depth, dtype=BF16)] * 3,
        in_specs=[VMEM] * 4,
        out_specs=[VMEM] * 4,
        cost_estimate=cost(8 * span * depth, 48 * span * depth),
        name="over_x",
    )


def to_y_kernel(place, block, up, far, down, gains, loss, message):
    span, depth = block.shape
    total = (block[...] + far[...].astype(F32)) + (up[...].astype(F32) + down[...].astype(F32))
    rows = span // SIDE
    extra = jnp.broadcast_to(loss[2:3, :1], (rows, TAIL))
    extra = jnp.concatenate([jnp.sum(gains[...], axis=0), extra], axis=1)
    for ds in range(SIDE):
        filled = jnp.concatenate([total[ds * rows : (ds + 1) * rows], extra], axis=1)
        message[lax.rem(place[0] + ds, SIDE)] = filled


def to_y(place, block, up, far, down, gains, loss, after=()):
    span, depth = block.shape
    return launch(
        to_y_kernel,
        (place, block, up, far, down, gains, loss),
        after,
        out_shape=shape(SIDE, span // SIDE, depth + gains.shape[2] + TAIL),
        in_specs=[SMEM] + [VMEM] * 6,
        out_specs=VMEM,
        cost_estimate=cost(8 * span * depth, 16 * span * depth),
        name="over_y",
    )


def finish_kernel(hidden, gain, message, out, gain_out, loss_out, dnormed):
    rows, width = hidden.shape
    depth = width // SIDE
    for s in range(SIDE):
        cut = pl.ds(s * depth, depth)
        dnormed[:, cut] = message[s, :, :depth]
        sums = message[s, :, depth:-TAIL]
        sums = jnp.concatenate([sums[i : i + 1] for i in range(rows)], axis=1)
        gain_out[:, cut] = sums / gain[:, cut]
    loss = message[:, 0, -TAIL:]
    loss_out[...] = jnp.sum(loss, axis=0, keepdims=True)
    values = hidden[...].astype(F32)
    inverse = lax.rsqrt(jnp.mean(values * values, axis=1, keepdims=True) + EPS)
    gained = dnormed[...] * gain[...]
    inner = jnp.mean(gained * values, axis=1, keepdims=True)
    out[...] = (inverse * gained - values * (inverse * inverse * inverse) * inner).astype(BF16)


def finish(hidden, gain, message, after=()):
    rows, width = hidden.shape
    return launch(
        finish_kernel,
        (hidden, gain, message),
        after,
        out_shape=[shape(rows, width, dtype=BF16), shape(1, width), shape(1, TAIL)],
        in_specs=[VMEM] * 3,
        out_specs=[VMEM] * 3,
        scratch_shapes=[pltpu.VMEM((rows, width), F32)],
        cost_estimate=cost(12 * rows * width, 16 * rows * width),
        name="finish",
    )


def section_weights(exit_layer, numerators):
    layers = numerators.shape[0]
    matches = exit_layer[:, None] == jnp.arange(layers, dtype=jnp.int32)[None, :]
    picked = jnp.sum(jnp.where(matches, numerators[None, :], 0), axis=1).astype(F32)
    return picked / jnp.sum(picked)


def local(hidden_rows, norm_gain, head_weight, targets, exit_layer, numerators):
    section, piece = lax.axis_index("section"), lax.axis_index("vocab")
    own_rows, width = hidden_rows.shape
    depth, columns = head_weight.shape
    place = jnp.stack([section, piece // 8, (piece // 2) % SIDE, piece % 2, piece * columns]).astype(jnp.int32)
    gain_row = norm_gain.reshape(1, width)
    weights = section_weights(exit_layer, numerators)
    weight = jnp.sum(jnp.where(jnp.arange(SIDE) == section, weights, 0.0)).reshape(1)

    cuts = normalise(place, in_hbm(hidden_rows), in_hbm(gain_row), targets)
    own = jnp.stack([cuts[0], over_section(cuts[3], -1), over_section(cuts[2], 2), over_section(cuts[1], 1)])
    def along_x(x):
        return [x, over_vocab(x, dx=-1), over_vocab(x, dx=2), over_vocab(x, dx=1)]

    pair = jnp.stack([over_vocab(own, dz=-1), over_vocab(own, dz=1)], axis=1)
    mine = [jnp.concatenate(along_x(own), axis=1)]
    held_head, token = hold(head_weight, (own,))
    *pair, _ = lax.optimization_barrier((*along_x(pair), token))
    mine.append(jnp.stack(pair, axis=2).reshape(SIDE, -1, own.shape[2]))
    mine.append(over_vocab(mine[0], dz=2))
    theirs = [over_vocab(m, dc=1) for m in mine]
    pieces = (*mine, *theirs)
    groups = ((0,), (1, 3), (2,))
    everything = (sum(groups, ()),)

    up, down = logits_of((2,), pieces, held_head)
    head_ready, _ = lax.optimization_barrier((head_weight, up))
    other_head = over_vocab(head_ready, dc=1)
    first, last = logits_of((1, 3), pieces, held_head, (up,))
    up, down = over_section(up, 1), over_section(down, -1)
    first, last = pass_on(first, last, up, down)
    (kept,) = logits_of((0,), pieces, held_head, (first,))
    below, above = over_section(first, 1), over_section(last, -1)
    exps, stats = own_logits(place, kept, below, above, mine, theirs)

    below, above = over_section(exps, 1), over_section(exps, -1)
    held_other, token = hold(other_head, (stats,))
    parts = pack(place, [stats], everything, own_rows, (token,))
    parts = merge([parts, over_vocab(parts, dc=1)])
    parts = merge(along_x(parts))
    far_first, far_last = halves(below, above, (parts, token))
    far_first, far_last = over_section(far_first, 1), over_section(far_last, -1)
    parts = [parts, over_vocab(parts, dz=-1), over_vocab(parts, dz=2), over_vocab(parts, dz=1)]
    scales = combine(place, weight, parts, stats, everything[0], own_rows)
    loss = scales
    scales = [scales, over_section(scales, -1), over_section(scales, 2), over_section(scales, 1)]

    others = dlogit_of(1, place, scales, exps, above, far_last, below, theirs, (far_first,))
    swapped = over_vocab(others, dc=1)
    ours = dlogit_of(0, place, scales, exps, above, far_first, below, mine, (others,))
    span = mine[0].shape[1]
    kept, to_up, to_down, to_far, gain = dnormed_of(ours, swapped, held_head, held_other, mine, span)
    moved = [over_vocab(to_far, dz=2), over_vocab(to_up, dz=1), over_vocab(to_down, dz=-1)]
    gains = lax.all_to_all(spread(gain), "vocab", 0, 0)
    head_grad, token = head_grad_of(pieces, ours, others, depth, (gain,))
    block, *cuts = to_x(kept, *moved, (token,))
    cuts = [over_vocab(cuts[0], dx=1), over_vocab(cuts[1], dx=2), over_vocab(cuts[2], dx=-1)]
    got = lax.all_to_all(to_y(place, block, *cuts, gains, loss), "section", 0, 0)
    hidden_grad, gain_grad, total_loss = finish(hidden_rows, gain_row, got)
    return (hidden_grad, gain_grad.reshape(width), head_grad, total_loss[0, 0])


def solution(mesh):
    return jax.shard_map(
        local,
        mesh=mesh,
        in_specs=(
            P(("section", "vocab"), None),
            P(),
            P("section", "vocab"),
            P(("section", "vocab")),
            P(),
            P(),
        ),
        out_specs=(P(("section", "vocab"), None), P(), P("section", "vocab"), P()),
        check_vma=False,
    )
```

```python
import functools
import jax
import jax.numpy as jnp
from jax import lax
from jax.experimental import pallas as pl
from jax.experimental.pallas import tpu as pltpu
from jax.sharding import PartitionSpec as P

EPS = 1e-05
SIDE = 4
TAIL = 128
TILE = 256
F32 = jnp.float32
BF16 = jnp.bfloat16
ANY = pl.BlockSpec(memory_space=pl.ANY)
VMEM = pl.BlockSpec(memory_space=pltpu.VMEM)
SMEM = pl.BlockSpec(memory_space=pltpu.SMEM)
PARAMS = pltpu.CompilerParams(vmem_limit_bytes=22 * 2**20)


def over_section(x, step):
    return lax.ppermute(x, "section", [(i, (i + step) % SIDE) for i in range(SIDE)])


def over_vocab(x, dx=0, dz=0, dc=0):
    pairs = []
    for px in range(SIDE):
        for pz in range(SIDE):
            for pc in range(2):
                to = (((px + dx) % SIDE) * SIDE + (pz + dz) % SIDE) * 2 + (pc ^ dc)
                pairs.append(((px * SIDE + pz) * 2 + pc, to))
    return lax.ppermute(x, "vocab", pairs)


def shape(*dims, dtype=F32):
    return jax.ShapeDtypeStruct(dims, dtype)


def cost(flops, moved):
    return pl.CostEstimate(flops=flops, bytes_accessed=moved, transcendentals=0)


def in_vmem(x):
    return pltpu.with_memory_space_constraint(x, pltpu.VMEM)


def in_hbm(x):
    return pltpu.with_memory_space_constraint(x, pltpu.HBM)


def launch(kernel, operands, after=(), *, in_specs, scratch_shapes=(), name, **options):
    used, ignored = len(operands), len(after)

    def body(*refs):
        kernel(*refs[:used], *refs[used + ignored :])

    return pl.pallas_call(
        body,
        in_specs=[*in_specs, *[ANY] * ignored],
        scratch_shapes=list(scratch_shapes),
        compiler_params=PARAMS,
        name=name,
        **options,
    )(*operands, *after)


def encode(x, message, at):
    rows, width = x.shape
    largest = jnp.max(jnp.abs(x), axis=1, keepdims=True)
    power = jnp.clip(jnp.floor(jnp.log2(jnp.maximum(largest, 1e-30))) + 1.0, -100.0, 100.0)
    codes = jnp.clip(jnp.round(x * jnp.exp2(15.0 - power)), -32767.0, 32767.0)
    message[pl.ds(at, rows), :width] = codes.astype(jnp.int32).astype(jnp.int16)
    tail = jnp.broadcast_to(power, (rows, TAIL)).astype(jnp.int32)
    message[pl.ds(at, rows), width:] = tail.astype(jnp.int16)


def decode(message, at, rows):
    width = message.shape[1] - TAIL
    power = message[pl.ds(at, rows), width:].astype(jnp.int32).astype(F32)[:, :1]
    codes = message[pl.ds(at, rows), :width].astype(jnp.int32).astype(F32)
    return codes * jnp.exp2(power - 15.0)


def hold_kernel(head, held, token, sem):
    copy = pltpu.make_async_copy(head, held, sem)
    copy.start()
    token[...] = jnp.zeros_like(token)
    copy.wait()


def hold(head, after=()):
    return launch(
        hold_kernel,
        (head,),
        after,
        out_shape=[pltpu.VMEM(head.shape, head.dtype), shape(8, TAIL)],
        in_specs=[ANY],
        out_specs=[VMEM] * 2,
        scratch_shapes=[pltpu.SemaphoreType.DMA(())],
        cost_estimate=cost(0, 2 * head.size),
        name="hold_head",
    )


def normalise_kernel(place, hidden, gain, targets, *blocks):
    rows, width = hidden.shape
    depth = width // SIDE
    values = hidden[...].astype(F32)
    inverse = lax.rsqrt(jnp.mean(values * values, axis=1, keepdims=True) + EPS)
    lane = lax.broadcasted_iota(jnp.int32, (rows, TAIL), 1)
    row = lax.broadcasted_iota(jnp.int32, (rows, TAIL), 0)
    digits = jnp.zeros((rows, TAIL), jnp.int32)
    for i in range(rows):
        high = targets[i] // 256
        low = targets[i] - high * 256
        digits = jnp.where(row == i, jnp.where(lane == 0, high, jnp.where(lane == 1, low, 0)), digits)
    digits = digits.astype(F32).astype(BF16)
    for step in range(SIDE):
        at = pl.multiple_of(lax.rem(place[0] + step, SIDE) * depth, depth)
        cut = hidden[:, pl.ds(at, depth)].astype(F32) * inverse * gain[:, pl.ds(at, depth)]
        blocks[step][:, :depth] = cut.astype(BF16)
        blocks[step][:, depth:] = digits


def normalise(place, hidden, gain, targets, after=()):
    rows, width = hidden.shape
    return launch(
        normalise_kernel,
        (place, hidden, gain, targets,),
        after,
        out_shape=[shape(rows, width // SIDE + TAIL, dtype=BF16)] * SIDE,
        in_specs=[SMEM, VMEM, VMEM, SMEM],
        out_specs=[VMEM] * SIDE,
        cost_estimate=cost(10 * rows * width, 8 * rows * width),
        name="normalise",
    )


def logits_kernel(offsets, count, *refs):
    pieces, head, refs = refs[:count], refs[count], refs[count + 1 :]
    depth, columns = head.shape
    outs, (rows, sems) = refs[:2], refs[-2:]
    per = rows.shape[1]
    step = pl.program_id(0)

    @pl.when(step == 0)
    def _():
        copies = []
        for i, ds in enumerate(offsets):
            at = 0
            for piece in pieces:
                span = piece.shape[1]
                to = rows.at[i, pl.ds(at, span), :]
                sem = sems.at[len(copies)]
                copies.append(pltpu.make_async_copy(piece.at[ds, :, pl.ds(0, depth)], to, sem))
                at += span
        for copy in copies:
            copy.start()
        for copy in copies:
            copy.wait()

    cut = pl.ds(pl.multiple_of(step * TILE, TILE), TILE)
    part = jnp.dot(rows[...].reshape(-1, depth), head[:, cut], preferred_element_type=F32)
    if offsets != (2,):
        for i in range(len(offsets)):
            outs[i][...] = part[i * per : (i + 1) * per]
        return
    far = refs[2]
    far[:, cut] = part

    @pl.when(step == pl.num_programs(0) - 1)
    def _():
        half = per // 2
        for at in range(0, half, 32):
            encode(far[pl.ds(at, 32), :], outs[0], at)
            encode(far[pl.ds(half + at, 32), :], outs[1], at)


def logits_of(offsets, pieces, head, after=()):
    depth, columns = head.shape
    count, per = len(offsets), sum(p.shape[1] for p in pieces)
    if offsets == (2,):
        outs = [shape(per // 2, columns + TAIL, dtype=jnp.int16)] * 2
        specs = [pl.BlockSpec((per // 2, columns + TAIL), lambda j: (0, 0))] * 2
        scratch = [pltpu.VMEM((per, columns), F32)]
    else:
        outs = [shape(per, columns)] * count
        specs = [pl.BlockSpec((per, TILE), lambda j: (0, j))] * count
        scratch = []
    scratch += [pltpu.VMEM((count, per, depth), BF16), pltpu.SemaphoreType.DMA((count * len(pieces),))]
    kernel = functools.partial(logits_kernel, offsets, len(pieces))
    if count == 1 and offsets != (2,):
        def kernel(*refs):
            at = len(pieces) + 1
            logits_kernel(offsets, len(pieces), *refs[: at + 1], None, *refs[at + 1 :])

    return launch(
        kernel,
        (*pieces, in_vmem(head)),
        after,
        grid=(columns // TILE,),
        out_shape=outs,
        in_specs=[ANY] * len(pieces) + [VMEM],
        out_specs=specs,
        scratch_shapes=scratch,
        cost_estimate=cost(0, 2 * depth * columns + 4 * count * per * columns),
        name="partial_logits",
    )


def pass_on_kernel(first, last, up, down, to_first, to_last):
    per = first.shape[0]
    half = per // 2
    for at in range(0, half, 32):
        encode(first[pl.ds(at, 32), :] + decode(up, at, 32), to_first, at)
        encode(last[pl.ds(at, 32), :], to_last, at)
        encode(first[pl.ds(half + at, 32), :], to_first, half + at)
        encode(last[pl.ds(half + at, 32), :] + decode(down, at, 32), to_last, half + at)


def pass_on(first, last, up, down, after=()):
    per, columns = first.shape
    return launch(
        pass_on_kernel,
        (first, last, up, down,),
        after,
        out_shape=[shape(per, columns + TAIL, dtype=jnp.int16)] * 2,
        in_specs=[VMEM] * 4,
        out_specs=[VMEM] * 2,
        cost_estimate=cost(20 * per * columns, 14 * per * columns),
        name="pass_on",
    )


def onehot_of(place, digits, columns):
    want = digits[:, :1].astype(F32) * 256.0 + digits[:, 1:2].astype(F32)
    want = want.astype(jnp.int32) - place[4]
    return lax.broadcasted_iota(jnp.int32, (digits.shape[0], columns), 1) == want


def own_logits_kernel(count, place, own, below, above, *refs):
    digits, exps, stats = refs[: 2 * count], refs[2 * count : -1], refs[-1]
    per, columns = own.shape
    at = 0
    for digit in digits:
        span = digit.shape[1]
        lane = lax.broadcasted_iota(jnp.int32, (span, TAIL), 1)
        x = own[pl.ds(at, span), :] + (decode(below, at, span) + decode(above, at, span))
        top = jnp.max(x, axis=1, keepdims=True)
        exp = jnp.exp(x - top)
        exps[at // (per // 2)][pl.ds(at % (per // 2), span), :] = exp.astype(BF16)
        total = jnp.sum(exp, axis=1, keepdims=True)
        pick = jnp.sum(jnp.where(onehot_of(place, digit[0], columns), x, 0.0), axis=1, keepdims=True)
        stats[pl.ds(at, span), :] = jnp.where(lane == 0, top, jnp.where(lane == 1, total, pick))
        at += span


def digit_specs(pieces):
    at = pieces[0].shape[2] // TAIL - 1
    return [pl.BlockSpec((1, p.shape[1], TAIL), lambda j: (0, 0, at)) for p in pieces]


def own_logits(place, own, below, above, mine, theirs, after=()):
    per, columns = own.shape
    full = pl.BlockSpec((per, columns), lambda j: (0, 0))
    coded = pl.BlockSpec((per, columns + TAIL), lambda j: (0, 0))
    return launch(
        functools.partial(own_logits_kernel, len(mine)),
        (place, own, below, above, *mine, *theirs),
        after,
        grid=(1,),
        out_shape=[shape(per // 2, columns, dtype=BF16)] * 2 + [shape(per, TAIL)],
        in_specs=[SMEM, full, coded, coded] + digit_specs([*mine, *theirs]),
        out_specs=[pl.BlockSpec((per // 2, columns), lambda j: (0, 0))] * 2 + [pl.BlockSpec((per, TAIL), lambda j: (0, 0))],
        cost_estimate=cost(20 * per * columns, 12 * per * columns),
        name="own_logits",
    )


def at_owner(place, dz, dc, dx, size):
    z = lax.rem(place[2] + dz, SIDE)
    x = lax.rem(place[1] + dx, SIDE)
    c = lax.rem(place[3] + dc, 2)
    return pl.multiple_of(((z * 2 + c) * SIDE + x) * size, size)


def walk(groups, size):
    for g, offsets in enumerate(groups):
        at = 0
        for dc in range(2):
            for dz in offsets:
                for dx in range(SIDE):
                    yield g, at, dz, dc, dx
                    at += size


def pack_kernel(groups, size, place, *refs):
    stats, (message, ordered) = refs[: len(groups)], refs[len(groups) :]
    for g, at, dz, dc, dx in walk(groups, size):
        ordered[pl.ds(at_owner(place, dz, dc, dx, size), size), :] = stats[g][pl.ds(at, size), :]
    message[...] = jnp.transpose(ordered[...])[:8]


def pack(place, stats, groups, size, after=()):
    rows = sum(s.shape[0] for s in stats)
    return launch(
        functools.partial(pack_kernel, groups, size),
        (place, *stats,),
        after,
        out_shape=shape(8, rows),
        in_specs=[SMEM] + [VMEM] * len(stats),
        out_specs=VMEM,
        scratch_shapes=[pltpu.VMEM((rows, TAIL), F32)],
        cost_estimate=cost(rows * TAIL, rows * TAIL * 4),
        name="pack_statistics",
    )


def merged(stats):
    tops = [x[:1] for x in stats]
    top = functools.reduce(jnp.maximum, tops)
    totals = [x[1:2] * jnp.exp(t - top) for x, t in zip(stats, tops)]
    picks = [x[2:3] for x in stats]
    if len(stats) == 4:
        totals, picks = ([x[0] + x[2], x[1] + x[3]] for x in (totals, picks))
    return top, totals[0] + totals[1], picks[0] + picks[1]


def merge_kernel(*refs):
    top, total, pick = merged([ref[...] for ref in refs[:-1]])
    row = lax.broadcasted_iota(jnp.int32, refs[-1].shape, 0)
    refs[-1][...] = jnp.where(row == 0, top, jnp.where(row == 1, total, pick))


def merge(stats, after=()):
    return launch(
        merge_kernel,
        (*stats,),
        after,
        out_shape=shape(*stats[0].shape),
        in_specs=[VMEM] * len(stats),
        out_specs=VMEM,
        cost_estimate=cost(64 * stats[0].size, 32 * stats[0].size),
        name="merge_statistics",
    )


def combine_kernel(offsets, size, count, place, weight, *refs):
    parts, (stats, message, ordered, scale) = refs[:count], refs[count:]
    top, total, pick = merged([ref[...] for ref in parts])
    log_total = top + jnp.log(total)
    loss = weight[0] * jnp.sum(log_total - pick, axis=1, keepdims=True)
    ordered[...] = jnp.transpose(jnp.broadcast_to(log_total, (TAIL, log_total.shape[1])))
    for _, at, dz, dc, dx in walk((offsets,), size):
        rows = ordered[pl.ds(at_owner(place, dz, dc, dx, size), size), :]
        scale[pl.ds(at, size), :] = weight[0] * jnp.exp(stats[pl.ds(at, size), :1] - rows)
    scales = jnp.transpose(scale[...])[:8]
    row = lax.broadcasted_iota(jnp.int32, scales.shape, 0)
    message[...] = jnp.where(row == 0, scales, jnp.where(row == 1, weight[0], loss))


def combine(place, weight, parts, stats, offsets, size, after=()):
    rows = stats.shape[0]
    return launch(
        functools.partial(combine_kernel, offsets, size, len(parts)),
        (place, weight, *parts, stats),
        after,
        out_shape=shape(8, rows),
        in_specs=[SMEM, SMEM] + [VMEM] * (len(parts) + 1),
        out_specs=VMEM,
        scratch_shapes=[pltpu.VMEM((rows, TAIL), F32)] * 2,
        cost_estimate=cost(rows * TAIL, rows * TAIL * 4),
        name="combine_statistics",
    )


def dlogit_kernel(dc, place, *refs):
    scales, (own, above, far, below), digits, out = refs[:SIDE], refs[SIDE : 2 * SIDE], refs[2 * SIDE : -1], refs[-1]
    half, columns = far.shape
    for ds in range(SIDE):
        scale = jnp.transpose(jnp.broadcast_to(scales[ds][:1], (TAIL, 2 * half)))
        weight = scales[ds][1:2, :1]
        at = 0
        for digit in digits:
            span = digit.shape[1]
            exp = (own, above, far, below)[ds][pl.ds(at, span), :]
            hit = onehot_of(place, digit[ds], columns)
            factor = scale[dc * half + at : dc * half + at + span, :1]
            grad = exp.astype(F32) * factor - jnp.where(hit, weight, 0.0)
            out[ds, pl.ds(at, span), :] = grad.astype(BF16)
            at += span


def dlogit_of(dc, place, scales, own, above, far, below, pieces, after=()):
    half, columns = far.shape
    at = pieces[0].shape[2] // TAIL - 1
    return launch(
        functools.partial(dlogit_kernel, dc),
        (place, *scales, own, above, far, below, *pieces),
        after,
        grid=(1,),
        out_shape=shape(SIDE, half, columns, dtype=BF16),
        in_specs=[SMEM]
        + [pl.BlockSpec(scales[0].shape, lambda j: (0, 0))] * SIDE
        + [pl.BlockSpec((half, columns), lambda j: (0, 0))] * 4
        + [pl.BlockSpec((SIDE, p.shape[1], TAIL), lambda j: (0, 0, at)) for p in pieces],
        out_specs=pl.BlockSpec((SIDE, half, columns), lambda j: (0, 0, 0)),
        cost_estimate=cost(40 * half * columns, 16 * half * columns),
        name="dlogit",
    )


def dnormed_kernel(count, left, right, head, other, *refs):
    normed, outs, gain = refs[: -1 - count], refs[-1 - count : -1], refs[-1]
    columns = head.shape[1]
    dims = (((1,), (1,)), ((), ()))
    cut = pl.ds(pl.multiple_of(pl.program_id(0) * TILE, TILE), TILE)
    part = lax.dot_general(left[...].reshape(-1, columns), head[cut, :], dims, preferred_element_type=F32)
    part = part + lax.dot_general(
        right[...].reshape(-1, columns), other[cut, :], dims, preferred_element_type=F32
    )
    x = jnp.concatenate([n[...] for n in normed], axis=1).reshape(part.shape).astype(F32)
    gain[...] = jnp.sum((part * x).reshape(-1, 8, TILE), axis=0)
    part = part.reshape(SIDE, count, -1, TILE)
    for k in range(count):
        outs[k][...] = part[:, k].astype(outs[k].dtype)


def dnormed_of(left, right, head, other, normed, span, after=()):
    depth, columns = head.shape
    count = sum(n.shape[1] for n in normed) // span
    block = pl.BlockSpec((SIDE, span, TILE), lambda j: (0, 0, j))
    return launch(
        functools.partial(dnormed_kernel, count),
        (left, right, in_vmem(head), in_vmem(other), *normed),
        after,
        grid=(depth // TILE,),
        out_shape=[shape(SIDE, span, depth, dtype=BF16 if k else F32) for k in range(count)] + [shape(8, depth)],
        in_specs=[VMEM] * 4 + [pl.BlockSpec((SIDE, n.shape[1], TILE), lambda j: (0, 0, j)) for n in normed],
        out_specs=[block] * count + [pl.BlockSpec((8, TILE), lambda j: (0, j))],
        cost_estimate=cost(0, 4 * depth * columns),
        name="dnormed",
    )


def head_grad_kernel(count, *refs):
    pieces, (ours, others) = refs[:count], refs[count : count + 2]
    out, token, grads, sems = refs[-4:]
    token[...] = jnp.zeros_like(token)

    @pl.when(pl.program_id(0) == 0)
    def _():
        copies = [(ours, grads.at[:, 0]), (others, grads.at[:, 1])]
        copies = [pltpu.make_async_copy(a, b, sems.at[i]) for i, (a, b) in enumerate(copies)]
        for copy in copies:
            copy.start()
        for copy in copies:
            copy.wait()

    x = jnp.concatenate([piece[...] for piece in pieces], axis=1).reshape(-1, TILE)
    y = grads[...].reshape(x.shape[0], -1)
    out[...] = lax.dot_general(x, y, (((0,), (0,)), ((), ())), preferred_element_type=F32).astype(BF16)


def head_grad_of(pieces, ours, others, depth, after=()):
    columns, rows = ours.shape[2], 2 * SIDE * ours.shape[1]
    return launch(
        functools.partial(head_grad_kernel, len(pieces)),
        tuple(in_hbm(x) for x in (*pieces, ours, others)),
        after,
        grid=(depth // TILE,),
        out_shape=[shape(depth, columns, dtype=BF16), shape(8, TAIL)],
        in_specs=[pl.BlockSpec((SIDE, p.shape[1], TILE), lambda j: (0, 0, j)) for p in pieces] + [ANY] * 2,
        out_specs=[pl.BlockSpec((TILE, columns), lambda j: (j, 0)), pl.BlockSpec((8, TAIL), lambda j: (0, 0))],
        scratch_shapes=[pltpu.VMEM((SIDE, 2, *ours.shape[1:]), BF16), pltpu.SemaphoreType.DMA((2,))],
        cost_estimate=cost(2 * rows * depth * columns, 2 * depth * columns + 4 * rows * depth),
        name="head_grad",
    )


def spread_kernel(terms, out):
    gain = jnp.sum(terms[...], axis=0, keepdims=True)
    wide = out.shape[2]
    gain = jnp.concatenate([gain[:, i * wide : (i + 1) * wide] for i in range(out.shape[1])], axis=0)
    out[...] = jnp.broadcast_to(gain, out.shape)


def spread(terms, after=()):
    rows, depth = terms.shape
    return launch(
        spread_kernel,
        (terms,),
        after,
        out_shape=shape(8 * SIDE, rows, depth // rows),
        in_specs=[VMEM],
        out_specs=VMEM,
        cost_estimate=cost(rows * depth, 4 * 8 * SIDE * depth),
        name="gain_parts",
    )


def to_x_kernel(own, far, up, down, block, *messages):
    total = (own[...] + far[...].astype(F32)) + (up[...].astype(F32) + down[...].astype(F32))
    rows = own.shape[1] // SIDE
    for dx in range(SIDE):
        cut = jnp.concatenate([total[ds, dx * rows : (dx + 1) * rows] for ds in range(SIDE)], axis=0)
        if dx == 0:
            block[...] = cut
        else:
            messages[dx - 1][...] = cut.astype(BF16)


def to_x(own, far, up, down, after=()):
    _, span, depth = own.shape
    return launch(
        to_x_kernel,
        (own, far, up, down),
        after,
        out_shape=[shape(span, depth)] + [shape(span, depth, dtype=BF16)] * 3,
        in_specs=[VMEM] * 4,
        out_specs=[VMEM] * 4,
        cost_estimate=cost(8 * span * depth, 48 * span * depth),
        name="over_x",
    )


def to_y_kernel(place, block, up, far, down, gains, loss, message):
    span, depth = block.shape
    total = (block[...] + far[...].astype(F32)) + (up[...].astype(F32) + down[...].astype(F32))
    rows = span // SIDE
    extra = jnp.broadcast_to(loss[2:3, :1], (rows, TAIL))
    extra = jnp.concatenate([jnp.sum(gains[...], axis=0), extra], axis=1)
    for ds in range(SIDE):
        filled = jnp.concatenate([total[ds * rows : (ds + 1) * rows], extra], axis=1)
        message[lax.rem(place[0] + ds, SIDE)] = filled


def to_y(place, block, up, far, down, gains, loss, after=()):
    span, depth = block.shape
    return launch(
        to_y_kernel,
        (place, block, up, far, down, gains, loss),
        after,
        out_shape=shape(SIDE, span // SIDE, depth + gains.shape[2] + TAIL),
        in_specs=[SMEM] + [VMEM] * 6,
        out_specs=VMEM,
        cost_estimate=cost(8 * span * depth, 16 * span * depth),
        name="over_y",
    )


def finish_kernel(hidden, gain, message, out, gain_out, loss_out, dnormed):
    rows, width = hidden.shape
    depth = width // SIDE
    for s in range(SIDE):
        cut = pl.ds(s * depth, depth)
        dnormed[:, cut] = message[s, :, :depth]
        sums = message[s, :, depth:-TAIL]
        sums = jnp.concatenate([sums[i : i + 1] for i in range(rows)], axis=1)
        gain_out[:, cut] = sums / gain[:, cut]
    loss = message[:, 0, -TAIL:]
    loss_out[...] = jnp.sum(loss, axis=0, keepdims=True)
    values = hidden[...].astype(F32)
    inverse = lax.rsqrt(jnp.mean(values * values, axis=1, keepdims=True) + EPS)
    gained = dnormed[...] * gain[...]
    inner = jnp.mean(gained * values, axis=1, keepdims=True)
    out[...] = (inverse * gained - values * (inverse * inverse * inverse) * inner).astype(BF16)


def finish(hidden, gain, message, after=()):
    rows, width = hidden.shape
    return launch(
        finish_kernel,
        (hidden, gain, message),
        after,
        out_shape=[shape(rows, width, dtype=BF16), shape(1, width), shape(1, TAIL)],
        in_specs=[VMEM] * 3,
        out_specs=[VMEM] * 3,
        scratch_shapes=[pltpu.VMEM((rows, width), F32)],
        cost_estimate=cost(12 * rows * width, 16 * rows * width),
        name="finish",
    )


def section_weights(exit_layer, numerators):
    layers = numerators.shape[0]
    matches = exit_layer[:, None] == jnp.arange(layers, dtype=jnp.int32)[None, :]
    picked = jnp.sum(jnp.where(matches, numerators[None, :], 0), axis=1).astype(F32)
    return picked / jnp.sum(picked)


def local(hidden_rows, norm_gain, head_weight, targets, exit_layer, numerators):
    section, piece = lax.axis_index("section"), lax.axis_index("vocab")
    own_rows, width = hidden_rows.shape
    depth, columns = head_weight.shape
    place = jnp.stack([section, piece // 8, (piece // 2) % SIDE, piece % 2, piece * columns]).astype(jnp.int32)
    gain_row = norm_gain.reshape(1, width)
    weights = section_weights(exit_layer, numerators)
    weight = jnp.sum(jnp.where(jnp.arange(SIDE) == section, weights, 0.0)).reshape(1)

    cuts = normalise(place, in_hbm(hidden_rows), in_hbm(gain_row), targets)
    held_head, token = hold(head_weight, (cuts[0],))
    *cuts, _ = lax.optimization_barrier(
        (cuts[0], over_section(cuts[3], -1), over_section(cuts[2], 2), over_section(cuts[1], 1), token)
    )
    own = jnp.stack(cuts)
    def along_x(x):
        return [x, over_vocab(x, dx=-1), over_vocab(x, dx=2), over_vocab(x, dx=1)]

    pair = jnp.stack([over_vocab(own, dz=-1), over_vocab(own, dz=1)], axis=1)
    mine = [jnp.concatenate(along_x(own), axis=1)]
    mine.append(jnp.stack(along_x(pair), axis=2).reshape(SIDE, -1, own.shape[2]))
    mine.append(over_vocab(mine[0], dz=2))
    theirs = [over_vocab(m, dc=1) for m in mine]
    pieces = (*mine, *theirs)
    groups = ((0,), (1, 3), (2,))
    everything = (sum(groups, ()),)

    up, down = logits_of((2,), pieces, held_head)
    head_ready, _ = lax.optimization_barrier((head_weight, up))
    other_head = over_vocab(head_ready, dc=1)
    first, last = logits_of((1, 3), pieces, held_head, (up,))
    up, down = over_section(up, 1), over_section(down, -1)
    first, last = pass_on(first, last, up, down)
    (kept,) = logits_of((0,), pieces, held_head, (first,))
    below, above = over_section(first, 1), over_section(last, -1)
    *exps, stats = own_logits(place, kept, below, above, mine, theirs)

    below_0, above_1 = over_section(exps[0], 1), over_section(exps[1], -1)
    below_1, above_0 = over_section(exps[1], 1), over_section(exps[0], -1)
    far_0, far_1 = over_section(below_0, 1), over_section(above_1, -1)
    held_other, token = hold(other_head, (stats,))
    parts = pack(place, [stats], everything, own_rows, (token,))
    parts = merge([parts, over_vocab(parts, dc=1)])
    parts = merge(along_x(parts))
    parts = [parts, over_vocab(parts, dz=-1), over_vocab(parts, dz=2), over_vocab(parts, dz=1)]
    scales = combine(place, weight, parts, stats, everything[0], own_rows)
    loss = scales
    scales = [scales, over_section(scales, -1), over_section(scales, 2), over_section(scales, 1)]

    others = dlogit_of(1, place, scales, exps[1], above_1, far_1, below_1, theirs, (far_0,))
    swapped = over_vocab(others, dc=1)
    ours = dlogit_of(0, place, scales, exps[0], above_0, far_0, below_0, mine, (others,))
    span = mine[0].shape[1]
    kept, to_up, to_down, to_far, gain = dnormed_of(ours, swapped, held_head, held_other, mine, span)
    moved = [over_vocab(to_far, dz=2), over_vocab(to_up, dz=1), over_vocab(to_down, dz=-1)]
    gains = lax.all_to_all(spread(gain), "vocab", 0, 0)
    head_grad, token = head_grad_of(pieces, ours, others, depth, (gain,))
    block, *cuts = to_x(kept, *moved, (token,))
    cuts = [over_vocab(cuts[0], dx=1), over_vocab(cuts[1], dx=2), over_vocab(cuts[2], dx=-1)]
    got = lax.all_to_all(to_y(place, block, *cuts, gains, loss), "section", 0, 0)
    hidden_grad, gain_grad, total_loss = finish(hidden_rows, gain_row, got)
    return (hidden_grad, gain_grad.reshape(width), head_grad, total_loss[0, 0])


def solution(mesh):
    return jax.shard_map(
        local,
        mesh=mesh,
        in_specs=(
            P(("section", "vocab"), None),
            P(),
            P("section", "vocab"),
            P(("section", "vocab")),
            P(),
            P(),
        ),
        out_specs=(P(("section", "vocab"), None), P(), P("section", "vocab"), P()),
        check_vma=False,
    )
```
